512 devices in a mesh: rows: 64 (over z, x), cols: 8 (over y, core).
Axes of the slice: x: 4, y: 4, z: 16, core: 2. Of those that a mesh axis runs over, the one named last changes fastest.
Arguments:
- slab: float32 [8192, 16384], P('rows', 'cols'), may hold values from -200 to 200, as said below
Outputs:
- r_rows: float32 [192, 16384], P(None, 'cols')
- updated: float32 [8192, 16384], P('rows', 'cols')
The draws below stay inside these ranges and needn't reach their ends.
Inputs may be any that keep to these rules, and one draw needn't show every extreme that they name: `slab`: Real-valued activations; every panel has full column rank.
All inputs are finite; a program needn't handle non-finite values.
Results may differ from the reference program's by a relative error of at most 0.0003.
Values sent between devices are 32-bit elements; how exact they have to be, the bound alone decides.
A program may use at most 64 MiB of HBM per device.

```python
import math
import jax
import jax.numpy as jnp
from jax import lax

D = 16384
PANEL = 64
PANELS = 3
TOKENS = 8192
N_COLS = 8


def draw_slab(key, part):
    key_one, key_two, key_three = jax.random.split(jax.random.fold_in(key, 7), 3)
    position = jnp.arange(TOKENS, dtype=jnp.float32) / TOKENS
    noise = jnp.clip(jax.random.normal(key_one, (TOKENS, D), jnp.float32), -4.0, 4.0)
    growth = 3.0 ** position
    rowscale = jnp.exp(jax.random.uniform(key_two, (TOKENS, 1), jnp.float32, math.log(0.3), math.log(3.0)))
    colscale = jnp.exp(jax.random.uniform(key_three, (1, D), jnp.float32, math.log(0.3), math.log(3.0)))
    return noise * rowscale * growth[:, None] * colscale


def setup_inputs(seed: int = 0) -> dict:
    key_list = jax.random.split(jax.random.key(seed), 2)
    slab = draw_slab(jax.random.fold_in(key_list[1], 71), 0)
    return {"slab": slab}


def reference(slab):
    current = slab
    col_count = D // N_COLS
    blocks = []
    for turn in range(PANELS):
        first_col = turn % N_COLS * col_count + turn // N_COLS * PANEL
        panel_cols = current[:, first_col:first_col + PANEL]
        basis, upper = jnp.linalg.qr(panel_cols)
        basis = basis * jnp.sign(jnp.diagonal(upper))[None, :]
        coeffs = jnp.dot(basis.T, current, precision=lax.Precision.HIGHEST)
        current = current - jnp.dot(basis, coeffs, precision=lax.Precision.HIGHEST)
        blocks.append(coeffs / jnp.sqrt(jnp.float32(TOKENS)))
    return (jnp.concatenate(blocks, 0), current)
```

```python
import functools
import math

import jax
import jax.numpy as jnp
from jax import lax
from jax.experimental import pallas as pl
from jax.experimental.pallas import tpu as pltpu
from jax.sharding import PartitionSpec as P

MESH = pl.DeviceIdType.MESH
PANEL = 64
PANELS = 3
N = PANEL * PANELS
F32 = jnp.float32


def dot(a, b, dims=((1,), (0,))):
    return lax.dot_general(
        a, b, (dims, ((), ())), precision=lax.Precision.HIGHEST, preferred_element_type=F32
    )


def dot_t(a, b):
    return dot(a, b, ((1,), (1,)))


def eliminate(s_ref):
    n = PANEL
    lane = lax.broadcasted_iota(jnp.int32, (n, n), 1)
    sub = lax.broadcasted_iota(jnp.int32, (n, n), 0)
    row_lane = lax.broadcasted_iota(jnp.int32, (1, n), 1)
    col_sub = lax.broadcasted_iota(jnp.int32, (n, 1), 0)

    def pick(value, where):
        return jnp.sum(jnp.where(where, value, 0.0), axis=1, keepdims=True)

    def step(i, _):
        j = 2 * i
        s = s_ref[...]
        r0 = s_ref[pl.ds(j, 1), :]
        r1 = s_ref[pl.ds(j + 1, 1), :]
        a = pick(r0, row_lane == j)
        b = pick(r1, row_lane == j)
        d = pick(r1, row_lane == j + 1)
        c0 = pick(s, lane == j)
        c1 = pick(s, lane == j + 1)
        a_inv = 1.0 / a
        ratio = b * a_inv
        second = d - b * ratio
        second_inv = 1.0 / second
        r0m = jnp.where(row_lane == j, 1.0, r0)
        r1n = jnp.where(row_lane == j, 0.0, r1) - ratio * r0m
        r0u = jnp.where(row_lane == j + 1, 0.0, r0m) * a_inv
        r1u = jnp.where(row_lane == j + 1, 1.0, r1n) * second_inv
        r1s = jnp.where(row_lane == j + 1, second, r1n)
        below = col_sub > j + 1
        c0b = jnp.where(below, c0, 0.0)
        c1b = jnp.where(below, c1 - c0 * ratio, 0.0)
        base = jnp.where((lane >= j) & (lane <= j + 1) & (sub > j + 1), 0.0, s)
        s_ref[...] = jnp.where(sub == j + 1, r1s, base - c0b * r0u - c1b * r1u)
        return 0

    lax.fori_loop(0, n // 2, step, 0)
    s = s_ref[...]
    pivots = pick(s, lane == sub)
    return jnp.where(lane < sub, s, jnp.where(lane == sub, 1.0, 0.0)) * (1.0 / jnp.sqrt(pivots))


def kernel(
    slab, r_out, u_out,
    at, gp, g1, g2, g3, gfull,
    mx, mz, rx1, rz1a, rz1b, rz1c, px, pz, rx2a, rx2b, rx2c, rz2, rr, mfx, mfz,
    s_ref, l_ref, t_ref, q_ref,
    p_send, p_recv, sends, recvs,
):
    row, col = lax.axis_index("rows"), lax.axis_index("cols")
    z, x = row // 4, row % 4
    zhi, zlo = z // 4, z % 4

    def at_z(dz):
        return (((z + dz + 16) % 16) * 4 + x, col)

    def at_x(d):
        return (z * 4 + (x + d) % 4, col)

    def at_col(d):
        return (row, (col + d) % 8)

    z_peers = (1, -1, 2, -2, 3, -3, 4, -4, 8)
    peers = [at_z(d) for d in z_peers] + [at_x(d) for d in (1, 2, 3)] + [at_col(d) for d in range(1, 8)]
    barrier = pltpu.get_barrier_semaphore()
    for peer in peers:
        pl.semaphore_signal(barrier, inc=1, device_id=peer, device_id_type=MESH)
    pl.semaphore_wait(barrier, len(peers))

    started = []

    def send(src, dst, peer):
        i = len(started)
        copy = pltpu.make_async_remote_copy(
            src_ref=src, dst_ref=dst, send_sem=sends.at[i], recv_sem=recvs.at[i],
            device_id=peer, device_id_type=MESH,
        )
        copy.start()
        started.append(copy)
        return copy

    def arrived(copies):
        for copy in copies:
            copy.wait_recv()

    def panel_copy(owner, d):
        rows = at.at[pl.ds(pl.multiple_of(owner * PANEL, PANEL), PANEL)]
        return pltpu.make_async_remote_copy(
            src_ref=rows, dst_ref=rows, send_sem=p_send.at[d - 1], recv_sem=p_recv.at[owner],
            device_id=at_col(d), device_id_type=MESH,
        )

    @pl.when(col < PANELS)
    def _():
        at[pl.ds(pl.multiple_of(col * PANEL, PANEL), PANEL), :] = slab[:, 0:128].T[:PANEL]
        for d in (4, 3, 5, 2, 6, 7, 1):
            panel_copy(col, d).start()

    for k in range(PANELS):
        @pl.when(col != k)
        def _():
            panel_copy(k, 1).wait_recv()

    panels_t = at[...]

    gp[0:24] = dot_t(panels_t, panels_t[0:128]).reshape(24, 8, 128)
    gp[24:32] = dot_t(panels_t[128:192], jnp.concatenate([panels_t[128:192], panels_t[128:192]], 0)).reshape(8, 8, 128)
    mine = 4 * col + x
    c_g1 = [send(gp.at[4 * col + (x + d) % 4], g1.at[d - 1], at_x(d)) for d in (2, 1, 3)]

    for q in range(4):
        mz[:, 256 * q:256 * q + 256] = dot(panels_t, slab[:, 1024 + 256 * q:1280 + 256 * q])

    def around_z(piece, half_a, half_b, dst, dst_a, dst_b):
        far = (zlo + 2) % 4
        return [
            send(half_a(far), dst_a, at_z(2)),
            send(half_b(far), dst_b, at_z(-2)),
            send(piece((zlo + 1) % 4), dst[0], at_z(1)),
            send(piece((zlo + 3) % 4), dst[1], at_z(-1)),
        ]

    def rows48(i):
        return pl.ds(pl.multiple_of(48 * i, 8), 48)

    def rows24(i, half):
        return pl.ds(pl.multiple_of(48 * i + 24 * half, 8), 24)

    c_z1 = around_z(
        lambda i: mz.at[rows48(i)], lambda i: mz.at[rows24(i, 0)], lambda i: mz.at[rows24(i, 1)],
        (rz1a, rz1b), rz1c.at[0:24], rz1c.at[24:48],
    )
    c_x1 = []
    for d in (2, 1, 3, 0):
        chunk = (x + d) % 4
        mx[chunk] = dot(panels_t, slab[:, pl.ds(pl.multiple_of(256 * chunk, 256), 256)])
        if d:
            c_x1.append(send(mx.at[chunk], rx1.at[d - 1], at_x(d)))

    arrived(c_g1)
    g2[zlo] = gp[mine] + g1[0] + g1[1] + g1[2]
    c_g2 = [
        send(g2.at[zlo], g2.at[zlo], ((zhi * 4 + (zlo + e) % 4) * 4 + x, col)) for e in (2, 1, 3)
    ]

    arrived(c_z1)
    for q in range(4):
        cols = slice(256 * q, 256 * q + 256)
        pz[q] = mz[rows48(zlo), cols] + rz1a[:, cols] + rz1b[:, cols] + rz1c[:, cols]
    arrived(c_g2)
    g3[zhi] = g2[0] + g2[1] + g2[2] + g2[3]
    c_g3 = [send(g3.at[zhi], g3.at[zhi], at_z(4 * e)) for e in (2, 1, 3)]
    c_z2 = [send(pz.at[(x + d) % 4], rz2.at[d - 1], at_x(d)) for d in (2, 1, 3)]

    arrived(c_x1)
    px[...] = mx[x] + rx1[0] + rx1[1] + rx1[2]
    c_x2 = around_z(
        lambda i: px.at[rows48(i)], lambda i: px.at[rows24(i, 0)], lambda i: px.at[rows24(i, 1)],
        (rx2a, rx2b), rx2c.at[0:24], rx2c.at[24:48],
    )

    arrived(c_z2)
    rr[1, zhi] = pz[x] + rz2[0] + rz2[1] + rz2[2]
    c_z3 = [send(rr.at[1, zhi], rr.at[1, zhi], at_z(4 * e)) for e in (2, 1, 3)]
    arrived(c_x2)
    rr[0, zhi] = px[rows48(zlo), :] + rx2a[...] + rx2b[...] + rx2c[...]
    c_x3 = [send(rr.at[0, zhi], rr.at[0, zhi], at_z(4 * e)) for e in (2, 1, 3)]

    arrived(c_g3)
    gfull[mine] = g3[0] + g3[1] + g3[2] + g3[3]
    c_g4 = [send(gfull.at[mine], gfull.at[mine], at_x(d)) for d in (2, 1, 3)]
    arrived(c_g4)
    four = gfull.at[pl.ds(4 * col, 4)]
    c_g5 = [send(four, four, at_col(d)) for d in (4, 3, 5, 2, 6, 7, 1)]
    arrived(c_g5)

    def block(i, j):
        if j == 2:
            return gfull[24:32].reshape(64, 128)[:, 0:64]
        return gfull[8 * i:8 * i + 8].reshape(64, 128)[:, 64 * j:64 * j + 64]

    t_ref[...] = jnp.zeros_like(t_ref)
    s_ref[...] = block(0, 0)
    t00 = eliminate(s_ref)
    l10, l20 = dot_t(block(1, 0), t00), dot_t(block(2, 0), t00)
    t_ref[0:64, 0:64] = t00
    l_ref[0], l_ref[1] = l10, l20
    s_ref[...] = block(1, 1) - dot_t(l10, l10)
    l_ref[2] = block(2, 1) - dot_t(l20, l10)
    l_ref[3] = block(2, 2) - dot_t(l20, l20)

    arrived(c_z3)
    wz = rr[1, 0] + rr[1, 1] + rr[1, 2] + rr[1, 3]
    mfz[x, rows48(zlo), :] = wz
    own = mfz.at[x, rows48(zlo)]
    c_z4 = [send(own, own, at_x(d)) for d in (2, 1, 3)]
    arrived(c_x3)
    mfx[x, rows48(zlo), :] = rr[0, 0] + rr[0, 1] + rr[0, 2] + rr[0, 3]

    def own_rows(ref):
        return around_z(
            lambda i: ref.at[rows48(zlo)], lambda i: ref.at[rows24(zlo, 0)], lambda i: ref.at[rows24(zlo, 1)],
            (ref.at[rows48(zlo)], ref.at[rows48(zlo)]), ref.at[rows24(zlo, 0)], ref.at[rows24(zlo, 1)],
        )

    c_x4 = own_rows(mfx.at[x])

    t11 = eliminate(s_ref)
    t_ref[64:128, 64:128] = t11
    l21 = dot_t(l_ref[2], t11)
    l_ref[2] = l21
    s_ref[...] = l_ref[3] - dot_t(l21, l21)

    arrived(c_z4)
    c_z5 = []
    far = mfz.at[:, rows24(zlo, 0)]
    c_z5.append(send(far, far, at_z(2)))
    far = mfz.at[:, rows24(zlo, 1)]
    c_z5.append(send(far, far, at_z(-2)))
    near = mfz.at[:, rows48(zlo)]
    c_z5.append(send(near, near, at_z(1)))
    c_z5.append(send(near, near, at_z(-1)))
    arrived(c_x4)
    c_x5 = [send(mfx.at[x], mfx.at[x], at_x(d)) for d in (2, 1, 3)]

    t22 = eliminate(s_ref)
    t00, t11 = t_ref[0:64, 0:64], t_ref[64:128, 64:128]
    l10, l20, l21 = l_ref[0], l_ref[1], l_ref[2]
    t10 = -dot(t11, dot(l10, t00))
    t_ref[64:128, 0:64] = t10
    t_ref[128:192, 0:64] = -dot(t22, dot(l20, t00) + dot(l21, t10))
    t_ref[128:192, 64:128] = -dot(t22, dot(l21, t11))
    t_ref[128:192, 128:192] = t22
    q_ref[...] = dot(t_ref[...], at[...]).T

    norm_scale = 1.0 / math.sqrt(128 * 64)

    def finish(chunk, first):
        cols = pl.ds(pl.multiple_of(first, 256), 256)
        coeffs = dot(t_ref[...], chunk)
        r_out[:, cols] = coeffs * norm_scale
        u_out[:, cols] = slab[:, cols] - dot(q_ref[...], coeffs)

    finish(mfx[x], 256 * x)
    for d, copy in zip((2, 1, 3), c_x5):
        copy.wait_recv()
    for d in (1, 2, 3):
        chunk = (x + d) % 4
        finish(mfx[chunk], 256 * chunk)
    arrived(c_z5)
    for q in range(4):
        finish(mfz[q], 1024 + 256 * q)

    for copy in started:
        copy.wait_send()

    @pl.when(col < PANELS)
    def _():
        for d in range(1, 8):
            panel_copy(col, d).wait_send()


MESSAGES = 53


def on_device(slab):
    vmem = pl.BlockSpec(memory_space=pltpu.VMEM)

    def buf(*shape):
        return pltpu.VMEM(shape, F32)

    return pl.pallas_call(
        kernel,
        out_shape=(
            jax.ShapeDtypeStruct((N, 2048), F32),
            jax.ShapeDtypeStruct((128, 2048), F32),
        ),
        in_specs=[vmem],
        out_specs=(vmem, vmem),
        scratch_shapes=[
            buf(N, 128), buf(32, 8, 128), buf(3, 8, 128), buf(4, 8, 128), buf(4, 8, 128), buf(32, 8, 128),
            buf(4, N, 256), buf(N, 1024), buf(3, N, 256), buf(48, 1024), buf(48, 1024), buf(48, 1024),
            buf(N, 256), buf(4, 48, 256), buf(48, 256), buf(48, 256), buf(48, 256), buf(3, 48, 256),
            buf(2, 4, 48, 256), buf(4, N, 256), buf(4, N, 256),
            buf(64, 64), buf(4, 64, 64), buf(N, N), buf(128, N),
            pltpu.SemaphoreType.DMA((7,)), pltpu.SemaphoreType.DMA((PANELS,)),
            pltpu.SemaphoreType.DMA((MESSAGES,)), pltpu.SemaphoreType.DMA((MESSAGES,)),
        ],
        compiler_params=pltpu.CompilerParams(
            collective_id=0, has_side_effects=True, vmem_limit_bytes=40 << 20
        ),
    )(slab)


def solution(mesh):
    return jax.shard_map(
        on_device,
        mesh=mesh,
        in_specs=(P("rows", "cols"),),
        out_specs=(P(None, "cols"), P("rows", "cols")),
        check_vma=False,
    )
```

```python
import functools
import math

import jax
import jax.numpy as jnp
from jax import lax
from jax.experimental import pallas as pl
from jax.experimental.pallas import tpu as pltpu
from jax.sharding import PartitionSpec as P

MESH = pl.DeviceIdType.MESH
PANEL = 64
PANELS = 3
N = PANEL * PANELS
F32 = jnp.float32


def dot(a, b, dims=((1,), (0,))):
    return lax.dot_general(
        a, b, (dims, ((), ())), precision=lax.Precision.HIGHEST, preferred_element_type=F32
    )


def dot_t(a, b):
    return dot(a, b, ((1,), (1,)))


def eliminate(s_ref):
    n = PANEL
    lane = lax.broadcasted_iota(jnp.int32, (n, n), 1)
    sub = lax.broadcasted_iota(jnp.int32, (n, n), 0)
    row_lane = lax.broadcasted_iota(jnp.int32, (1, n), 1)
    col_sub = lax.broadcasted_iota(jnp.int32, (n, 1), 0)

    def pick(value, where):
        return jnp.sum(jnp.where(where, value, 0.0), axis=1, keepdims=True)

    def step(i, _):
        j = 2 * i
        s = s_ref[...]
        r0 = s_ref[pl.ds(j, 1), :]
        r1 = s_ref[pl.ds(j + 1, 1), :]
        a = pick(r0, row_lane == j)
        b = pick(r1, row_lane == j)
        d = pick(r1, row_lane == j + 1)
        c0 = pick(s, lane == j)
        c1 = pick(s, lane == j + 1)
        a_inv = 1.0 / a
        ratio = b * a_inv
        second = d - b * ratio
        second_inv = 1.0 / second
        r0m = jnp.where(row_lane == j, 1.0, r0)
        r1n = jnp.where(row_lane == j, 0.0, r1) - ratio * r0m
        r0u = jnp.where(row_lane == j + 1, 0.0, r0m) * a_inv
        r1u = jnp.where(row_lane == j + 1, 1.0, r1n) * second_inv
        r1s = jnp.where(row_lane == j + 1, second, r1n)
        below = col_sub > j + 1
        c0b = jnp.where(below, c0, 0.0)
        c1b = jnp.where(below, c1 - c0 * ratio, 0.0)
        base = jnp.where((lane >= j) & (lane <= j + 1) & (sub > j + 1), 0.0, s)
        s_ref[...] = jnp.where(sub == j + 1, r1s, base - c0b * r0u - c1b * r1u)
        return 0

    lax.fori_loop(0, n // 2, step, 0)
    s = s_ref[...]
    pivots = pick(s, lane == sub)
    return jnp.where(lane < sub, s, jnp.where(lane == sub, 1.0, 0.0)) * (1.0 / jnp.sqrt(pivots))


def kernel(
    slab_hbm, r_out, u_out,
    slab, r_buf, u_buf, at, gp, g1, g2, g3, gfull,
    mx, mz, rx1, rz1a, rz1b, rz1c, px, pz, rx2a, rx2b, rx2c, rz2, rr, mfx, mfz,
    s_ref, l_ref, t_ref, q_ref,
    p_send, p_recv, sends, recvs, in_sem, out_sem, far1, far2,
):
    row, col = lax.axis_index("rows"), lax.axis_index("cols")
    z, x = row // 4, row % 4
    zhi, zlo = z // 4, z % 4

    def at_z(dz):
        return (((z + dz + 16) % 16) * 4 + x, col)

    def at_x(d):
        return (z * 4 + (x + d) % 4, col)

    def at_col(d):
        return (row, (col + d) % 8)

    first = pltpu.make_async_copy(slab_hbm.at[:, 0:256], slab.at[:, 0:256], in_sem.at[0])
    rest = pltpu.make_async_copy(slab_hbm.at[:, 256:2048], slab.at[:, 256:2048], in_sem.at[1])
    first.start()
    rest.start()

    z_peers = (1, -1, 2, -2, 3, -3)
    peers = [at_z(d) for d in z_peers] + [at_x(d) for d in (1, 2, 3)] + [at_col(d) for d in range(1, 8)]
    barrier = pltpu.get_barrier_semaphore()
    for peer in peers:
        pl.semaphore_signal(barrier, inc=1, device_id=peer, device_id_type=MESH)
    pl.semaphore_wait(barrier, len(peers))
    for d in (2, -2):
        pl.semaphore_signal(far1, inc=1, device_id=at_z(d), device_id_type=MESH)
    first.wait()

    started = []

    def send(src, dst, peer):
        i = len(started)
        copy = pltpu.make_async_remote_copy(
            src_ref=src, dst_ref=dst, send_sem=sends.at[i], recv_sem=recvs.at[i],
            device_id=peer, device_id_type=MESH,
        )
        copy.start()
        started.append(copy)
        return copy

    def arrived(copies):
        for copy in copies:
            copy.wait_recv()

    def panel_copy(owner, d):
        rows = at.at[pl.ds(pl.multiple_of(owner * PANEL, PANEL), PANEL)]
        return pltpu.make_async_remote_copy(
            src_ref=rows, dst_ref=rows, send_sem=p_send.at[d - 1], recv_sem=p_recv.at[owner],
            device_id=at_col(d), device_id_type=MESH,
        )

    @pl.when(col < PANELS)
    def _():
        at[pl.ds(pl.multiple_of(col * PANEL, PANEL), PANEL), :] = slab[:, 0:128].T[:PANEL]
        for d in (4, 3, 5, 2, 6, 7, 1):
            panel_copy(col, d).start()

    pl.semaphore_wait(far1, 2)
    for d in (4, -4):
        pl.semaphore_signal(far2, inc=1, device_id=at_z(d), device_id_type=MESH)
    rest.wait()
    for k in range(PANELS):
        @pl.when(col != k)
        def _():
            panel_copy(k, 1).wait_recv()

    panels_t = at[...]

    gp[0:24] = dot_t(panels_t, panels_t[0:128]).reshape(24, 8, 128)
    gp[24:32] = dot_t(panels_t[128:192], jnp.concatenate([panels_t[128:192], panels_t[128:192]], 0)).reshape(8, 8, 128)
    mine = 4 * col + x
    c_g1 = [send(gp.at[4 * col + (x + d) % 4], g1.at[d - 1], at_x(d)) for d in (2, 1, 3)]

    for q in range(4):
        mz[:, 256 * q:256 * q + 256] = dot(panels_t, slab[:, 1024 + 256 * q:1280 + 256 * q])

    def around_z(piece, half_a, half_b, dst, dst_a, dst_b):
        far = (zlo + 2) % 4
        return [
            send(half_a(far), dst_a, at_z(2)),
            send(half_b(far), dst_b, at_z(-2)),
            send(piece((zlo + 1) % 4), dst[0], at_z(1)),
            send(piece((zlo + 3) % 4), dst[1], at_z(-1)),
        ]

    def rows48(i):
        return pl.ds(pl.multiple_of(48 * i, 8), 48)

    def rows24(i, half):
        return pl.ds(pl.multiple_of(48 * i + 24 * half, 8), 24)

    c_z1 = around_z(
        lambda i: mz.at[rows48(i)], lambda i: mz.at[rows24(i, 0)], lambda i: mz.at[rows24(i, 1)],
        (rz1a, rz1b), rz1c.at[0:24], rz1c.at[24:48],
    )
    c_x1 = []
    for d in (2, 1, 3, 0):
        chunk = (x + d) % 4
        mx[chunk] = dot(panels_t, slab[:, pl.ds(pl.multiple_of(256 * chunk, 256), 256)])
        if d:
            c_x1.append(send(mx.at[chunk], rx1.at[d - 1], at_x(d)))

    arrived(c_g1)
    g2[zlo] = gp[mine] + g1[0] + g1[1] + g1[2]
    c_g2 = [
        send(g2.at[zlo], g2.at[zlo], ((zhi * 4 + (zlo + e) % 4) * 4 + x, col)) for e in (2, 1, 3)
    ]

    arrived(c_z1)
    for q in range(4):
        cols = slice(256 * q, 256 * q + 256)
        pz[q] = mz[rows48(zlo), cols] + rz1a[:, cols] + rz1b[:, cols] + rz1c[:, cols]
    arrived(c_g2)
    g3[zhi] = g2[0] + g2[1] + g2[2] + g2[3]
    pl.semaphore_wait(far2, 2)
    c_g3 = [send(g3.at[zhi], g3.at[zhi], at_z(4 * e)) for e in (2, 1, 3)]
    c_z2 = [send(pz.at[(x + d) % 4], rz2.at[d - 1], at_x(d)) for d in (2, 1, 3)]

    arrived(c_x1)
    px[...] = mx[x] + rx1[0] + rx1[1] + rx1[2]
    c_x2 = around_z(
        lambda i: px.at[rows48(i)], lambda i: px.at[rows24(i, 0)], lambda i: px.at[rows24(i, 1)],
        (rx2a, rx2b), rx2c.at[0:24], rx2c.at[24:48],
    )

    arrived(c_z2)
    rr[1, zhi] = pz[x] + rz2[0] + rz2[1] + rz2[2]
    c_z3 = [send(rr.at[1, zhi], rr.at[1, zhi], at_z(4 * e)) for e in (2, 1, 3)]
    arrived(c_x2)
    rr[0, zhi] = px[rows48(zlo), :] + rx2a[...] + rx2b[...] + rx2c[...]
    c_x3 = [send(rr.at[0, zhi], rr.at[0, zhi], at_z(4 * e)) for e in (2, 1, 3)]

    arrived(c_g3)
    gfull[mine] = g3[0] + g3[1] + g3[2] + g3[3]
    c_g4 = [send(gfull.at[mine], gfull.at[mine], at_x(d)) for d in (2, 1, 3)]
    arrived(c_g4)
    four = gfull.at[pl.ds(4 * col, 4)]
    c_g5 = [send(four, four, at_col(d)) for d in (4, 3, 5, 2, 6, 7, 1)]
    arrived(c_g5)

    arrived(c_z3)
    wz = rr[1, 0] + rr[1, 1] + rr[1, 2] + rr[1, 3]
    mfz[x, rows48(zlo), :] = wz
    own = mfz.at[x, rows48(zlo)]
    c_z4 = [send(own, own, at_x(d)) for d in (2, 1, 3)]
    arrived(c_x3)
    mfx[x, rows48(zlo), :] = rr[0, 0] + rr[0, 1] + rr[0, 2] + rr[0, 3]

    def own_rows(ref, at_rows):
        whole, half_a, half_b = (at_rows(ref, rows) for rows in (rows48(zlo), rows24(zlo, 0), rows24(zlo, 1)))
        return around_z(
            lambda i: whole, lambda i: half_a, lambda i: half_b, (whole, whole), half_a, half_b
        )

    c_x4 = own_rows(mfx.at[x], lambda ref, rows: ref.at[rows])

    def block(i, j):
        if j == 2:
            return gfull[24:32].reshape(64, 128)[:, 0:64]
        return gfull[8 * i:8 * i + 8].reshape(64, 128)[:, 64 * j:64 * j + 64]

    t_ref[...] = jnp.zeros_like(t_ref)
    s_ref[...] = block(0, 0)
    t00 = eliminate(s_ref)
    l10, l20 = dot_t(block(1, 0), t00), dot_t(block(2, 0), t00)
    t_ref[0:64, 0:64] = t00
    l_ref[0], l_ref[1] = l10, l20
    s_ref[...] = block(1, 1) - dot_t(l10, l10)
    l_ref[2] = block(2, 1) - dot_t(l20, l10)
    l_ref[3] = block(2, 2) - dot_t(l20, l20)

    arrived(c_z4)
    c_z5 = []
    for half in (slice(0, 2), slice(2, 4)):
        c_z5.append(own_rows(mfz.at[half], lambda ref, rows: ref.at[:, rows]))
    arrived(c_x4)
    c_x5 = [send(mfx.at[x], mfx.at[x], at_x(d)) for d in (2, 1, 3)]

    t11 = eliminate(s_ref)
    t_ref[64:128, 64:128] = t11
    l21 = dot_t(l_ref[2], t11)
    l_ref[2] = l21
    s_ref[...] = l_ref[3] - dot_t(l21, l21)

    t22 = eliminate(s_ref)
    t00, t11 = t_ref[0:64, 0:64], t_ref[64:128, 64:128]
    l10, l20, l21 = l_ref[0], l_ref[1], l_ref[2]
    t10 = -dot(t11, dot(l10, t00))
    t_ref[64:128, 0:64] = t10
    t_ref[128:192, 0:64] = -dot(t22, dot(l20, t00) + dot(l21, t10))
    t_ref[128:192, 64:128] = -dot(t22, dot(l21, t11))
    t_ref[128:192, 128:192] = t22
    q_ref[...] = dot(t_ref[...], at[...]).T

    norm_scale = 1.0 / math.sqrt(128 * 64)

    outs = []

    def finish(chunk, first):
        i = len(outs) // 2
        cols = pl.ds(pl.multiple_of(first, 256), 256)
        coeffs = dot(t_ref[...], chunk)
        r_buf[i] = coeffs * norm_scale
        outs.append(pltpu.make_async_copy(r_buf.at[i], r_out.at[:, cols], out_sem.at[2 * i]))
        outs[-1].start()
        u_buf[i] = slab[:, cols] - dot(q_ref[...], coeffs)
        outs.append(pltpu.make_async_copy(u_buf.at[i], u_out.at[:, cols], out_sem.at[2 * i + 1]))
        outs[-1].start()

    finish(mfx[x], 256 * x)
    for half in range(2):
        arrived(c_z5[half])
        for q in (2 * half, 2 * half + 1):
            finish(mfz[q], 1024 + 256 * q)
    for i, d in ((1, 1), (2, 3), (0, 2)):
        c_x5[i].wait_recv()
        chunk = (x + 4 - d) % 4
        finish(mfx[chunk], 256 * chunk)

    for copy in outs:
        copy.wait()
    for copy in started:
        copy.wait_send()

    @pl.when(col < PANELS)
    def _():
        for d in range(1, 8):
            panel_copy(col, d).wait_send()


MESSAGES = 57


def on_device(slab):
    hbm = pl.BlockSpec(memory_space=pltpu.HBM)
    place = pl.BlockSpec(memory_space=pl.ANY)

    def buf(*shape):
        return pltpu.VMEM(shape, F32)

    return pl.pallas_call(
        kernel,
        out_shape=(
            jax.ShapeDtypeStruct((N, 2048), F32),
            jax.ShapeDtypeStruct((128, 2048), F32),
        ),
        in_specs=[hbm],
        out_specs=(place, place),
        scratch_shapes=[
            buf(128, 2048), buf(8, N, 256), buf(8, 128, 256), buf(N, 128), buf(32, 8, 128), buf(3, 8, 128), buf(4, 8, 128), buf(4, 8, 128), buf(32, 8, 128),
            buf(4, N, 256), buf(N, 1024), buf(3, N, 256), buf(48, 1024), buf(48, 1024), buf(48, 1024),
            buf(N, 256), buf(4, 48, 256), buf(48, 256), buf(48, 256), buf(48, 256), buf(3, 48, 256),
            buf(2, 4, 48, 256), buf(4, N, 256), buf(4, N, 256),
            buf(64, 64), buf(4, 64, 64), buf(N, N), buf(128, N),
            pltpu.SemaphoreType.DMA((7,)), pltpu.SemaphoreType.DMA((PANELS,)),
            pltpu.SemaphoreType.DMA((MESSAGES,)), pltpu.SemaphoreType.DMA((MESSAGES,)),
            pltpu.SemaphoreType.DMA((2,)), pltpu.SemaphoreType.DMA((16,)),
            pltpu.SemaphoreType.REGULAR, pltpu.SemaphoreType.REGULAR,
        ],
        compiler_params=pltpu.CompilerParams(
            collective_id=0, has_side_effects=True, vmem_limit_bytes=48 << 20
        ),
    )(slab)


def solution(mesh):
    return jax.shard_map(
        on_device,
        mesh=mesh,
        in_specs=(P("rows", "cols"),),
        out_specs=(P(None, "cols"), P("rows", "cols")),
        check_vma=False,
    )
```

```python
import functools
import math

import jax
import jax.numpy as jnp
from jax import lax
from jax.experimental import pallas as pl
from jax.experimental.pallas import tpu as pltpu
from jax.sharding import PartitionSpec as P

MESH = pl.DeviceIdType.MESH
PANEL = 64
PANELS = 3
N = PANEL * PANELS
F32 = jnp.float32


def dot(a, b, dims=((1,), (0,))):
    return lax.dot_general(
        a, b, (dims, ((), ())), precision=lax.Precision.HIGHEST, preferred_element_type=F32
    )


def dot_t(a, b):
    return dot(a, b, ((1,), (1,)))


def eliminate(s_ref):
    n = PANEL
    lane = lax.broadcasted_iota(jnp.int32, (n, n), 1)
    sub = lax.broadcasted_iota(jnp.int32, (n, n), 0)
    row_lane = lax.broadcasted_iota(jnp.int32, (1, n), 1)
    col_sub = lax.broadcasted_iota(jnp.int32, (n, 1), 0)

    def pick(value, where):
        return jnp.sum(jnp.where(where, value, 0.0), axis=1, keepdims=True)

    def step(i, _):
        j = 2 * i
        s = s_ref[...]
        r0 = s_ref[pl.ds(j, 1), :]
        r1 = s_ref[pl.ds(j + 1, 1), :]
        a = pick(r0, row_lane == j)
        b = pick(r1, row_lane == j)
        d = pick(r1, row_lane == j + 1)
        c0 = pick(s, lane == j)
        c1 = pick(s, lane == j + 1)
        a_inv = 1.0 / a
        ratio = b * a_inv
        second = d - b * ratio
        second_inv = 1.0 / second
        r0m = jnp.where(row_lane == j, 1.0, r0)
        r1n = jnp.where(row_lane == j, 0.0, r1) - ratio * r0m
        r0u = jnp.where(row_lane == j + 1, 0.0, r0m) * a_inv
        r1u = jnp.where(row_lane == j + 1, 1.0, r1n) * second_inv
        r1s = jnp.where(row_lane == j + 1, second, r1n)
        below = col_sub > j + 1
        c0b = jnp.where(below, c0, 0.0)
        c1b = jnp.where(below, c1 - c0 * ratio, 0.0)
        base = jnp.where((lane >= j) & (lane <= j + 1) & (sub > j + 1), 0.0, s)
        s_ref[...] = jnp.where(sub == j + 1, r1s, base - c0b * r0u - c1b * r1u)
        return 0

    lax.fori_loop(0, n // 2, step, 0)
    s = s_ref[...]
    pivots = pick(s, lane == sub)
    return jnp.where(lane < sub, s, jnp.where(lane == sub, 1.0, 0.0)) * (1.0 / jnp.sqrt(pivots))


def kernel(
    slab_hbm, r_out, u_out,
    slab, r_buf, u_buf, at, gp, g1, g2, gfull,
    mx, mz, rx1, rz1a, rz1b, rz1c, px, pz, rx2a, rx2b, rx2c, rz2, rr, mfx, mfz, cx,
    s_ref, l_ref, t_ref, q_ref,
    p_send, p_recv, sends, recvs, in_sem, out_sem, far1, far2,
):
    row, col = lax.axis_index("rows"), lax.axis_index("cols")
    z, x = row // 4, row % 4
    zhi, zlo = z // 4, z % 4

    def at_z(dz):
        return (((z + dz + 16) % 16) * 4 + x, col)

    def at_x(d):
        return (z * 4 + (x + d) % 4, col)

    def at_col(d):
        return (row, (col + d) % 8)

    first = pltpu.make_async_copy(slab_hbm.at[:, 0:256], slab.at[:, 0:256], in_sem.at[0])
    rest = pltpu.make_async_copy(slab_hbm.at[:, 256:2048], slab.at[:, 256:2048], in_sem.at[1])
    first.start()
    rest.start()

    z_peers = (1, -1, 2, -2)
    peers = [at_z(d) for d in z_peers] + [at_x(d) for d in (1, 2, 3)] + [at_col(d) for d in range(1, 8)]
    barrier = pltpu.get_barrier_semaphore()
    for peer in peers:
        pl.semaphore_signal(barrier, inc=1, device_id=peer, device_id_type=MESH)
    pl.semaphore_wait(barrier, len(peers))
    for d in (2, -2):
        pl.semaphore_signal(far1, inc=1, device_id=at_z(d), device_id_type=MESH)
    first.wait()

    started = []

    def send(src, dst, peer):
        i = len(started)
        copy = pltpu.make_async_remote_copy(
            src_ref=src, dst_ref=dst, send_sem=sends.at[i], recv_sem=recvs.at[i],
            device_id=peer, device_id_type=MESH,
        )
        copy.start()
        started.append(copy)
        return copy

    def arrived(copies):
        for copy in copies:
            copy.wait_recv()

    def panel_copy(owner, d):
        rows = at.at[pl.ds(pl.multiple_of(owner * PANEL, PANEL), PANEL)]
        return pltpu.make_async_remote_copy(
            src_ref=rows, dst_ref=rows, send_sem=p_send.at[d - 1], recv_sem=p_recv.at[owner],
            device_id=at_col(d), device_id_type=MESH,
        )

    @pl.when(col < PANELS)
    def _():
        at[pl.ds(pl.multiple_of(col * PANEL, PANEL), PANEL), :] = slab[:, 0:128].T[:PANEL]
        for d in (4, 3, 5, 2, 6, 7, 1):
            panel_copy(col, d).start()

    pl.semaphore_wait(far1, 2)
    for d in (4, -4):
        pl.semaphore_signal(far2, inc=1, device_id=at_z(d), device_id_type=MESH)
    rest.wait()
    for k in range(PANELS):
        @pl.when(col != k)
        def _():
            panel_copy(k, 1).wait_recv()

    panels_t = at[...]

    gp[0:24] = dot_t(panels_t, panels_t[0:128]).reshape(24, 8, 128)
    gp[24:32] = dot_t(panels_t[128:192], jnp.concatenate([panels_t[128:192], panels_t[128:192]], 0)).reshape(8, 8, 128)
    mine = 4 * col + x
    c_g1 = [send(gp.at[4 * col + (x + d) % 4], g1.at[d - 1], at_x(d)) for d in (2, 1, 3)]

    def around_z(piece, half_a, half_b, dst, dst_a, dst_b):
        far = (zlo + 2) % 4
        return [
            send(half_a(far), dst_a, at_z(2)),
            send(half_b(far), dst_b, at_z(-2)),
            send(piece((zlo + 1) % 4), dst[0], at_z(1)),
            send(piece((zlo + 3) % 4), dst[1], at_z(-1)),
        ]

    def rows48(i):
        return pl.ds(pl.multiple_of(48 * i, 8), 48)

    def rows24(i, half):
        return pl.ds(pl.multiple_of(48 * i + 24 * half, 8), 24)

    def first_z(half):
        for q in (2 * half, 2 * half + 1):
            mz[:, 256 * q:256 * q + 256] = dot(panels_t, slab[:, 1024 + 256 * q:1280 + 256 * q])

    def send_z(half):
        cols = slice(512 * half, 512 * half + 512)
        return around_z(
            lambda i: mz.at[rows48(i), cols], lambda i: mz.at[rows24(i, 0), cols],
            lambda i: mz.at[rows24(i, 1), cols],
            (rz1a.at[:, cols], rz1b.at[:, cols]), rz1c.at[0:24, cols], rz1c.at[24:48, cols],
        )

    first_z(0)
    c_z1 = send_z(0)
    c_x1 = []
    for d in (2, 1, 3, 0):
        chunk = (x + d) % 4
        mx[chunk] = dot(panels_t, slab[:, pl.ds(pl.multiple_of(256 * chunk, 256), 256)])
        if d:
            c_x1.append(send(mx.at[chunk], rx1.at[d - 1], at_x(d)))
    first_z(1)

    arrived(c_g1)
    g2[z] = gp[mine] + g1[0] + g1[1] + g1[2]
    pl.semaphore_wait(far2, 2)
    c_g2 = [send(g2.at[z], g2.at[z], at_z(d)) for d in (8, 7, 9, 6, 10, 5, 11, 4, 12, 3, 13, 2, 14, 1, 15)]
    c_z1 += send_z(1)

    arrived(c_x1)
    px[...] = mx[x] + rx1[0] + rx1[1] + rx1[2]
    c_x2 = around_z(
        lambda i: px.at[rows48(i)], lambda i: px.at[rows24(i, 0)], lambda i: px.at[rows24(i, 1)],
        (rx2a, rx2b), rx2c.at[0:24], rx2c.at[24:48],
    )
    arrived(c_g2)
    total = g2[0]
    for i in range(1, 16):
        total = total + g2[i]
    gfull[mine] = total
    c_g4 = [send(gfull.at[mine], gfull.at[mine], at_x(d)) for d in (2, 1, 3)]
    arrived(c_z1)
    for q in range(4):
        cols = slice(256 * q, 256 * q + 256)
        pz[q] = mz[rows48(zlo), cols] + rz1a[:, cols] + rz1b[:, cols] + rz1c[:, cols]
    c_z2 = [send(pz.at[(x + d) % 4], rz2.at[d - 1], at_x(d)) for d in (2, 1, 3)]
    arrived(c_g4)
    four = gfull.at[pl.ds(4 * col, 4)]
    c_g5 = [send(four, four, at_col(d)) for d in (4, 3, 5, 2, 6, 7, 1)]
    arrived(c_x2)
    rr[0, zhi] = px[rows48(zlo), :] + rx2a[...] + rx2b[...] + rx2c[...]
    c_x3 = [send(rr.at[0, zhi], rr.at[0, zhi], at_z(4 * e)) for e in (2, 1, 3)]
    arrived(c_z2)
    rr[1, zhi] = pz[x] + rz2[0] + rz2[1] + rz2[2]
    c_z3 = [send(rr.at[1, zhi], rr.at[1, zhi], at_z(4 * e)) for e in (2, 1, 3)]
    arrived(c_g5)

    def block(i, j):
        if j == 2:
            return gfull[24:32].reshape(64, 128)[:, 0:64]
        return gfull[8 * i:8 * i + 8].reshape(64, 128)[:, 64 * j:64 * j + 64]

    t_ref[...] = jnp.zeros_like(t_ref)
    s_ref[...] = block(0, 0)
    t00 = eliminate(s_ref)
    l10, l20 = dot_t(block(1, 0), t00), dot_t(block(2, 0), t00)
    t_ref[0:64, 0:64] = t00
    l_ref[0], l_ref[1] = l10, l20
    s_ref[...] = block(1, 1) - dot_t(l10, l10)
    l_ref[2] = block(2, 1) - dot_t(l20, l10)
    l_ref[3] = block(2, 2) - dot_t(l20, l20)

    t11 = eliminate(s_ref)
    t_ref[64:128, 64:128] = t11
    l21 = dot_t(l_ref[2], t11)
    l_ref[2] = l21
    s_ref[...] = l_ref[3] - dot_t(l21, l21)

    def own_rows(ref, at_rows):
        whole, half_a, half_b = (at_rows(ref, rows) for rows in (rows48(zlo), rows24(zlo, 0), rows24(zlo, 1)))
        return around_z(
            lambda i: whole, lambda i: half_a, lambda i: half_b, (whole, whole), half_a, half_b
        )

    arrived(c_x3)
    mfx[x, rows48(zlo), :] = rr[0, 0] + rr[0, 1] + rr[0, 2] + rr[0, 3]
    c_x4 = own_rows(mfx.at[x], lambda ref, rows: ref.at[rows])
    arrived(c_z3)
    mfz[x, rows48(zlo), :] = rr[1, 0] + rr[1, 1] + rr[1, 2] + rr[1, 3]
    own = mfz.at[x, rows48(zlo)]
    c_z4 = [send(own, own, at_x(d)) for d in (2, 1, 3)]

    t22 = eliminate(s_ref)
    t00, t11 = t_ref[0:64, 0:64], t_ref[64:128, 64:128]
    l10, l20, l21 = l_ref[0], l_ref[1], l_ref[2]
    t10 = -dot(t11, dot(l10, t00))
    t_ref[64:128, 0:64] = t10
    t_ref[128:192, 0:64] = -dot(t22, dot(l20, t00) + dot(l21, t10))
    t_ref[128:192, 64:128] = -dot(t22, dot(l21, t11))
    t_ref[128:192, 128:192] = t22
    q_ref[...] = dot(t_ref[...], at[...]).T

    norm_scale = 1.0 / math.sqrt(128 * 64)

    arrived(c_z4)
    c_z5 = [own_rows(mfz.at[q], lambda ref, rows: ref.at[rows]) for q in range(4)]
    arrived(c_x4)
    cx[x] = dot(t_ref[...], mfx[x])
    c_x5 = [send(cx.at[x], cx.at[x], at_x(d)) for d in (2, 1, 3)]
    outs = []

    def finish(coeffs, first):
        i = len(outs) // 2
        cols = pl.ds(pl.multiple_of(first, 256), 256)
        r_buf[i] = coeffs * norm_scale
        outs.append(pltpu.make_async_copy(r_buf.at[i], r_out.at[:, cols], out_sem.at[2 * i]))
        outs[-1].start()
        u_buf[i] = slab[:, cols] - dot(q_ref[...], coeffs)
        outs.append(pltpu.make_async_copy(u_buf.at[i], u_out.at[:, cols], out_sem.at[2 * i + 1]))
        outs[-1].start()

    finish(cx[x], 256 * x)
    for q in range(4):
        arrived(c_z5[q])
        finish(dot(t_ref[...], mfz[q]), 1024 + 256 * q)
    for i, d in ((1, 1), (2, 3), (0, 2)):
        c_x5[i].wait_recv()
        chunk = (x + 4 - d) % 4
        finish(cx[chunk], 256 * chunk)

    for copy in outs:
        copy.wait()
    for copy in started:
        copy.wait_send()

    @pl.when(col < PANELS)
    def _():
        for d in range(1, 8):
            panel_copy(col, d).wait_send()


MESSAGES = 78


def on_device(slab):
    hbm = pl.BlockSpec(memory_space=pltpu.HBM)
    place = pl.BlockSpec(memory_space=pl.ANY)

    def buf(*shape):
        return pltpu.VMEM(shape, F32)

    return pl.pallas_call(
        kernel,
        out_shape=(
            jax.ShapeDtypeStruct((N, 2048), F32),
            jax.ShapeDtypeStruct((128, 2048), F32),
        ),
        in_specs=[hbm],
        out_specs=(place, place),
        scratch_shapes=[
            buf(128, 2048), buf(8, N, 256), buf(8, 128, 256), buf(N, 128), buf(32, 8, 128), buf(3, 8, 128), buf(16, 8, 128), buf(32, 8, 128),
            buf(4, N, 256), buf(N, 1024), buf(3, N, 256), buf(48, 1024), buf(48, 1024), buf(48, 1024),
            buf(N, 256), buf(4, 48, 256), buf(48, 256), buf(48, 256), buf(48, 256), buf(3, 48, 256),
            buf(2, 4, 48, 256), buf(4, N, 256), buf(4, N, 256), buf(4, N, 256),
            buf(64, 64), buf(4, 64, 64), buf(N, N), buf(128, N),
            pltpu.SemaphoreType.DMA((7,)), pltpu.SemaphoreType.DMA((PANELS,)),
            pltpu.SemaphoreType.DMA((MESSAGES,)), pltpu.SemaphoreType.DMA((MESSAGES,)),
            pltpu.SemaphoreType.DMA((2,)), pltpu.SemaphoreType.DMA((16,)),
            pltpu.SemaphoreType.REGULAR, pltpu.SemaphoreType.REGULAR,
        ],
        compiler_params=pltpu.CompilerParams(
            collective_id=0, has_side_effects=True, vmem_limit_bytes=63 << 20
        ),
    )(slab)


def solution(mesh):
    return jax.shard_map(
        on_device,
        mesh=mesh,
        in_specs=(P("rows", "cols"),),
        out_specs=(P(None, "cols"), P("rows", "cols")),
        check_vma=False,
    )
```

```python
import functools
import math

import jax
import jax.numpy as jnp
from jax import lax
from jax.experimental import pallas as pl
from jax.experimental.pallas import tpu as pltpu
from jax.sharding import PartitionSpec as P

MESH = pl.DeviceIdType.MESH
PANEL = 64
PANELS = 3
N = PANEL * PANELS
F32 = jnp.float32


def dot(a, b, dims=((1,), (0,))):
    return lax.dot_general(
        a, b, (dims, ((), ())), precision=lax.Precision.HIGHEST, preferred_element_type=F32
    )


def dot_t(a, b):
    return dot(a, b, ((1,), (1,)))


def eliminate(s_ref):
    n = PANEL
    lane = lax.broadcasted_iota(jnp.int32, (n, n), 1)
    sub = lax.broadcasted_iota(jnp.int32, (n, n), 0)
    row_lane = lax.broadcasted_iota(jnp.int32, (1, n), 1)
    col_sub = lax.broadcasted_iota(jnp.int32, (n, 1), 0)

    def pick(value, where):
        return jnp.sum(jnp.where(where, value, 0.0), axis=1, keepdims=True)

    def step(i, _):
        j = 2 * i
        s = s_ref[...]
        r0 = s_ref[pl.ds(j, 1), :]
        r1 = s_ref[pl.ds(j + 1, 1), :]
        a = pick(r0, row_lane == j)
        b = pick(r1, row_lane == j)
        d = pick(r1, row_lane == j + 1)
        c0 = pick(s, lane == j)
        c1 = pick(s, lane == j + 1)
        a_inv = 1.0 / a
        ratio = b * a_inv
        second = d - b * ratio
        second_inv = 1.0 / second
        r0m = jnp.where(row_lane == j, 1.0, r0)
        r1n = jnp.where(row_lane == j, 0.0, r1) - ratio * r0m
        r0u = jnp.where(row_lane == j + 1, 0.0, r0m) * a_inv
        r1u = jnp.where(row_lane == j + 1, 1.0, r1n) * second_inv
        r1s = jnp.where(row_lane == j + 1, second, r1n)
        below = col_sub > j + 1
        c0b = jnp.where(below, c0, 0.0)
        c1b = jnp.where(below, c1 - c0 * ratio, 0.0)
        base = jnp.where((lane >= j) & (lane <= j + 1) & (sub > j + 1), 0.0, s)
        s_ref[...] = jnp.where(sub == j + 1, r1s, base - c0b * r0u - c1b * r1u)
        return 0

    lax.fori_loop(0, n // 2, step, 0)
    s = s_ref[...]
    pivots = pick(s, lane == sub)
    return jnp.where(lane < sub, s, jnp.where(lane == sub, 1.0, 0.0)) * (1.0 / jnp.sqrt(pivots))


def kernel(
    slab_hbm, r_out, u_out,
    slab, r_buf, u_buf, at, gp, g1, g2, gfull,
    mx, mz, rx1, rz1a, rz1b, rz1c, px, pz, rx2a, rx2b, rx2c, rz2, rr, mfx, mfz, cx,
    s_ref, l_ref, t_ref, q_ref,
    p_send, p_recv, sends, recvs, in_sem, out_sem, far1, far2,
):
    row, col = lax.axis_index("rows"), lax.axis_index("cols")
    z, x = row // 4, row % 4
    zhi, zlo = z // 4, z % 4

    def at_z(dz):
        return (((z + dz + 16) % 16) * 4 + x, col)

    def at_x(d):
        return (z * 4 + (x + d) % 4, col)

    def at_col(d):
        return (row, (col + d) % 8)

    first = pltpu.make_async_copy(slab_hbm.at[:, 0:256], slab.at[:, 0:256], in_sem.at[0])
    rest = pltpu.make_async_copy(slab_hbm.at[:, 256:2048], slab.at[:, 256:2048], in_sem.at[1])
    first.start()
    rest.start()

    z_peers = (1, -1, 2, -2)
    peers = [at_z(d) for d in z_peers] + [at_x(d) for d in (1, 2, 3)] + [at_col(d) for d in range(1, 8)]
    barrier = pltpu.get_barrier_semaphore()
    for peer in peers:
        pl.semaphore_signal(barrier, inc=1, device_id=peer, device_id_type=MESH)
    pl.semaphore_wait(barrier, len(peers))
    for d in (2, -2):
        pl.semaphore_signal(far1, inc=1, device_id=at_z(d), device_id_type=MESH)
    first.wait()

    started = []

    def send(src, dst, peer):
        i = len(started)
        copy = pltpu.make_async_remote_copy(
            src_ref=src, dst_ref=dst, send_sem=sends.at[i], recv_sem=recvs.at[i],
            device_id=peer, device_id_type=MESH,
        )
        copy.start()
        started.append(copy)
        return copy

    def arrived(copies):
        for copy in copies:
            copy.wait_recv()

    def panel_copy(owner, d):
        rows = at.at[pl.ds(pl.multiple_of(owner * PANEL, PANEL), PANEL)]
        return pltpu.make_async_remote_copy(
            src_ref=rows, dst_ref=rows, send_sem=p_send.at[d - 1], recv_sem=p_recv.at[owner],
            device_id=at_col(d), device_id_type=MESH,
        )

    @pl.when(col < PANELS)
    def _():
        at[pl.ds(pl.multiple_of(col * PANEL, PANEL), PANEL), :] = slab[:, 0:128].T[:PANEL]
        for d in (4, 3, 5, 2, 6, 7, 1):
            panel_copy(col, d).start()

    pl.semaphore_wait(far1, 2)
    for d in (4, -4):
        pl.semaphore_signal(far2, inc=1, device_id=at_z(d), device_id_type=MESH)
    rest.wait()
    for k in range(PANELS):
        @pl.when(col != k)
        def _():
            panel_copy(k, 1).wait_recv()

    panels_t = at[...]

    gp[0:24] = dot_t(panels_t, panels_t[0:128]).reshape(24, 8, 128)
    gp[24:32] = dot_t(panels_t[128:192], jnp.concatenate([panels_t[128:192], panels_t[128:192]], 0)).reshape(8, 8, 128)
    mine = 4 * col + x
    c_g1 = [send(gp.at[4 * col + (x + d) % 4], g1.at[d - 1], at_x(d)) for d in (2, 1, 3)]

    def around_z(piece, half_a, half_b, dst, dst_a, dst_b):
        far = (zlo + 2) % 4
        return [
            send(half_a(far), dst_a, at_z(2)),
            send(half_b(far), dst_b, at_z(-2)),
            send(piece((zlo + 1) % 4), dst[0], at_z(1)),
            send(piece((zlo + 3) % 4), dst[1], at_z(-1)),
        ]

    def rows48(i):
        return pl.ds(pl.multiple_of(48 * i, 8), 48)

    def rows24(i, half):
        return pl.ds(pl.multiple_of(48 * i + 24 * half, 8), 24)

    def first_z(half):
        for q in (2 * half, 2 * half + 1):
            mz[:, 256 * q:256 * q + 256] = dot(panels_t, slab[:, 1024 + 256 * q:1280 + 256 * q])

    def send_z(half):
        cols = slice(512 * half, 512 * half + 512)
        return around_z(
            lambda i: mz.at[rows48(i), cols], lambda i: mz.at[rows24(i, 0), cols],
            lambda i: mz.at[rows24(i, 1), cols],
            (rz1a.at[:, cols], rz1b.at[:, cols]), rz1c.at[0:24, cols], rz1c.at[24:48, cols],
        )

    first_z(0)
    c_z1 = send_z(0)
    c_x1 = []
    for d in (2, 1, 3, 0):
        chunk = (x + d) % 4
        mx[chunk] = dot(panels_t, slab[:, pl.ds(pl.multiple_of(256 * chunk, 256), 256)])
        if d:
            c_x1.append(send(mx.at[chunk], rx1.at[d - 1], at_x(d)))
    first_z(1)

    arrived(c_g1)
    g2[z] = gp[mine] + g1[0] + g1[1] + g1[2]
    pl.semaphore_wait(far2, 2)
    c_g2 = [send(g2.at[z], g2.at[z], at_z(d)) for d in (8, 7, 9, 6, 10, 5, 11, 4, 12, 3, 13, 2, 14, 1, 15)]
    c_z1 += send_z(1)

    arrived(c_x1)
    px[...] = mx[x] + rx1[0] + rx1[1] + rx1[2]
    c_x2 = around_z(
        lambda i: px.at[rows48(i)], lambda i: px.at[rows24(i, 0)], lambda i: px.at[rows24(i, 1)],
        (rx2a, rx2b), rx2c.at[0:24], rx2c.at[24:48],
    )
    arrived(c_g2)
    total = g2[0]
    for i in range(1, 16):
        total = total + g2[i]
    gfull[mine] = total
    c_g4 = [send(gfull.at[mine], gfull.at[mine], at_x(d)) for d in (2, 1, 3)]
    arrived(c_z1)
    for q in range(4):
        cols = slice(256 * q, 256 * q + 256)
        pz[q] = mz[rows48(zlo), cols] + rz1a[:, cols] + rz1b[:, cols] + rz1c[:, cols]
    c_z2 = [send(pz.at[(x + d) % 4], rz2.at[d - 1], at_x(d)) for d in (2, 1, 3)]
    arrived(c_g4)
    four = gfull.at[pl.ds(4 * col, 4)]
    c_g5 = [send(four, four, at_col(d)) for d in (4, 3, 5, 2, 6, 7, 1)]
    arrived(c_x2)
    rr[0, zhi] = px[rows48(zlo), :] + rx2a[...] + rx2b[...] + rx2c[...]
    c_x3 = [send(rr.at[0, zhi], rr.at[0, zhi], at_z(4 * e)) for e in (2, 1, 3)]
    arrived(c_z2)
    rr[1, zhi] = pz[x] + rz2[0] + rz2[1] + rz2[2]
    c_z3 = [send(rr.at[1, zhi], rr.at[1, zhi], at_z(4 * e)) for e in (2, 1, 3)]
    arrived(c_g5)

    def block(i, j):
        if j == 2:
            return gfull[24:32].reshape(64, 128)[:, 0:64]
        return gfull[8 * i:8 * i + 8].reshape(64, 128)[:, 64 * j:64 * j + 64]

    t_ref[...] = jnp.zeros_like(t_ref)
    s_ref[...] = block(0, 0)
    t00 = eliminate(s_ref)
    l10, l20 = dot_t(block(1, 0), t00), dot_t(block(2, 0), t00)
    t_ref[0:64, 0:64] = t00
    l_ref[0], l_ref[1] = l10, l20
    s_ref[...] = block(1, 1) - dot_t(l10, l10)
    l_ref[2] = block(2, 1) - dot_t(l20, l10)
    l_ref[3] = block(2, 2) - dot_t(l20, l20)

    t11 = eliminate(s_ref)
    t_ref[64:128, 64:128] = t11
    l21 = dot_t(l_ref[2], t11)
    l_ref[2] = l21
    s_ref[...] = l_ref[3] - dot_t(l21, l21)

    def own_rows(ref, at_rows):
        whole, half_a, half_b = (at_rows(ref, rows) for rows in (rows48(zlo), rows24(zlo, 0), rows24(zlo, 1)))
        return around_z(
            lambda i: whole, lambda i: half_a, lambda i: half_b, (whole, whole), half_a, half_b
        )

    arrived(c_x3)
    mfx[x, rows48(zlo), :] = rr[0, 0] + rr[0, 1] + rr[0, 2] + rr[0, 3]
    c_x4 = own_rows(mfx.at[x], lambda ref, rows: ref.at[rows])
    arrived(c_z3)
    mfz[x, rows48(zlo), :] = rr[1, 0] + rr[1, 1] + rr[1, 2] + rr[1, 3]
    own = mfz.at[x, rows48(zlo)]
    c_z4 = [send(own, own, at_x(d)) for d in (2, 1, 3)]

    t22 = eliminate(s_ref)
    t00, t11 = t_ref[0:64, 0:64], t_ref[64:128, 64:128]
    l10, l20, l21 = l_ref[0], l_ref[1], l_ref[2]
    t10 = -dot(t11, dot(l10, t00))
    t_ref[64:128, 0:64] = t10
    t_ref[128:192, 0:64] = -dot(t22, dot(l20, t00) + dot(l21, t10))
    t_ref[128:192, 64:128] = -dot(t22, dot(l21, t11))
    t_ref[128:192, 128:192] = t22
    q_ref[...] = dot(t_ref[...], at[...]).T

    norm_scale = 1.0 / math.sqrt(128 * 64)

    arrived(c_z4)
    c_z5 = [own_rows(mfz.at[q], lambda ref, rows: ref.at[rows]) for q in range(4)]
    arrived(c_x4)
    cx[x] = dot(t_ref[...], mfx[x])
    c_x5 = [send(cx.at[x], cx.at[x], at_x(d)) for d in (2, 1, 3)]
    outs = []

    def finish(coeffs, first):
        i = len(outs) // 2
        cols = pl.ds(pl.multiple_of(first, 256), 256)
        r_buf[i] = coeffs * norm_scale
        outs.append(pltpu.make_async_copy(r_buf.at[i], r_out.at[:, cols], out_sem.at[2 * i]))
        outs[-1].start()
        u_buf[i] = slab[:, cols] - dot(q_ref[...], coeffs)
        outs.append(pltpu.make_async_copy(u_buf.at[i], u_out.at[:, cols], out_sem.at[2 * i + 1]))
        outs[-1].start()

    finish(cx[x], 256 * x)
    for q in range(4):
        arrived(c_z5[q])
        finish(dot(t_ref[...], mfz[q]), 1024 + 256 * q)
    for i, d in ((1, 1), (2, 3), (0, 2)):
        c_x5[i].wait_recv()
        chunk = (x + 4 - d) % 4
        finish(cx[chunk], 256 * chunk)

    for copy in outs:
        copy.wait()
    for copy in started:
        copy.wait_send()

    @pl.when(col < PANELS)
    def _():
        for d in range(1, 8):
            panel_copy(col, d).wait_send()


def write_out(r_in, u_in, r_out, u_out, sems):
    copies = [
        pltpu.make_async_copy(r_in, r_out, sems.at[0]),
        pltpu.make_async_copy(u_in, u_out, sems.at[1]),
    ]
    for copy in copies:
        copy.start()
    for copy in copies:
        copy.wait()


MESSAGES = 78


def on_device(slab):
    hbm = pl.BlockSpec(memory_space=pltpu.HBM)
    place = pl.BlockSpec(memory_space=pl.ANY)

    def buf(*shape):
        return pltpu.VMEM(shape, F32)

    results = pl.pallas_call(
        kernel,
        out_shape=(
            jax.ShapeDtypeStruct((N, 2048), F32),
            jax.ShapeDtypeStruct((128, 2048), F32),
        ),
        in_specs=[hbm],
        out_specs=(place, place),
        scratch_shapes=[
            buf(128, 2048), buf(8, N, 256), buf(8, 128, 256), buf(N, 128), buf(32, 8, 128), buf(3, 8, 128), buf(16, 8, 128), buf(32, 8, 128),
            buf(4, N, 256), buf(N, 1024), buf(3, N, 256), buf(48, 1024), buf(48, 1024), buf(48, 1024),
            buf(N, 256), buf(4, 48, 256), buf(48, 256), buf(48, 256), buf(48, 256), buf(3, 48, 256),
            buf(2, 4, 48, 256), buf(4, N, 256), buf(4, N, 256), buf(4, N, 256),
            buf(64, 64), buf(4, 64, 64), buf(N, N), buf(128, N),
            pltpu.SemaphoreType.DMA((7,)), pltpu.SemaphoreType.DMA((PANELS,)),
            pltpu.SemaphoreType.DMA((MESSAGES,)), pltpu.SemaphoreType.DMA((MESSAGES,)),
            pltpu.SemaphoreType.DMA((2,)), pltpu.SemaphoreType.DMA((16,)),
            pltpu.SemaphoreType.REGULAR, pltpu.SemaphoreType.REGULAR,
        ],
        compiler_params=pltpu.CompilerParams(
            collective_id=0, has_side_effects=True, vmem_limit_bytes=50 << 20
        ),
    )(slab)
    return pl.pallas_call(
        write_out,
        out_shape=(
            jax.ShapeDtypeStruct((N, 2048), F32),
            jax.ShapeDtypeStruct((128, 2048), F32),
        ),
        in_specs=[place, place],
        out_specs=(place, place),
        scratch_shapes=[pltpu.SemaphoreType.DMA((2,))],
        compiler_params=pltpu.CompilerParams(vmem_limit_bytes=8 << 20),
    )(*results)


def solution(mesh):
    return jax.shard_map(
        on_device,
        mesh=mesh,
        in_specs=(P("rows", "cols"),),
        out_specs=(P(None, "cols"), P("rows", "cols")),
        check_vma=False,
    )
```

```python
import functools
import math

import jax
import jax.numpy as jnp
from jax import lax
from jax.experimental import pallas as pl
from jax.experimental.pallas import tpu as pltpu
from jax.sharding import PartitionSpec as P

MESH = pl.DeviceIdType.MESH
PANEL = 64
PANELS = 3
N = PANEL * PANELS
F32 = jnp.float32


def dot(a, b, dims=((1,), (0,))):
    return lax.dot_general(
        a, b, (dims, ((), ())), precision=lax.Precision.HIGHEST, preferred_element_type=F32
    )


def dot_t(a, b):
    return dot(a, b, ((1,), (1,)))


def eliminate(s_ref):
    n = PANEL
    lane = lax.broadcasted_iota(jnp.int32, (n, n), 1)
    sub = lax.broadcasted_iota(jnp.int32, (n, n), 0)
    row_lane = lax.broadcasted_iota(jnp.int32, (1, n), 1)
    col_sub = lax.broadcasted_iota(jnp.int32, (n, 1), 0)

    def pick(value, where):
        return jnp.sum(jnp.where(where, value, 0.0), axis=1, keepdims=True)

    def step(i, _):
        j = 2 * i
        s = s_ref[...]
        r0 = s_ref[pl.ds(j, 1), :]
        r1 = s_ref[pl.ds(j + 1, 1), :]
        a = pick(r0, row_lane == j)
        b = pick(r1, row_lane == j)
        d = pick(r1, row_lane == j + 1)
        c0 = pick(s, lane == j)
        c1 = pick(s, lane == j + 1)
        a_inv = 1.0 / a
        ratio = b * a_inv
        second = d - b * ratio
        second_inv = 1.0 / second
        r0m = jnp.where(row_lane == j, 1.0, r0)
        r1n = jnp.where(row_lane == j, 0.0, r1) - ratio * r0m
        r0u = jnp.where(row_lane == j + 1, 0.0, r0m) * a_inv
        r1u = jnp.where(row_lane == j + 1, 1.0, r1n) * second_inv
        r1s = jnp.where(row_lane == j + 1, second, r1n)
        below = col_sub > j + 1
        c0b = jnp.where(below, c0, 0.0)
        c1b = jnp.where(below, c1 - c0 * ratio, 0.0)
        base = jnp.where((lane >= j) & (lane <= j + 1) & (sub > j + 1), 0.0, s)
        s_ref[...] = jnp.where(sub == j + 1, r1s, base - c0b * r0u - c1b * r1u)
        return 0

    lax.fori_loop(0, n // 2, step, 0)
    s = s_ref[...]
    pivots = pick(s, lane == sub)
    return jnp.where(lane < sub, s, jnp.where(lane == sub, 1.0, 0.0)) * (1.0 / jnp.sqrt(pivots))


def kernel(
    slab_hbm, r_out, u_out,
    slab, r_buf, u_buf, at, gp, g1, g2, gfull,
    mx, mz, rx1, rz1a, rz1b, rz1c, px, pz, rx2a, rx2b, rx2c, rz2, rr, mfx, mfz, cx,
    s_ref, l_ref, t_ref, q_ref,
    p_send, p_recv, sends, recvs, in_sem, out_sem, far1, far2,
):
    row, col = lax.axis_index("rows"), lax.axis_index("cols")
    z, x = row // 4, row % 4
    zhi, zlo = z // 4, z % 4

    def at_z(dz):
        return (((z + dz + 16) % 16) * 4 + x, col)

    def at_x(d):
        return (z * 4 + (x + d) % 4, col)

    def at_col(d):
        return (row, (col + d) % 8)

    first = pltpu.make_async_copy(slab_hbm.at[:, 0:256], slab.at[:, 0:256], in_sem.at[0])
    rest = pltpu.make_async_copy(slab_hbm.at[:, 256:2048], slab.at[:, 256:2048], in_sem.at[1])
    first.start()
    rest.start()

    z_peers = (1, -1, 2, -2)
    peers = [at_z(d) for d in z_peers] + [at_x(d) for d in (1, 2, 3)] + [at_col(d) for d in range(1, 8)]
    barrier = pltpu.get_barrier_semaphore()
    for peer in peers:
        pl.semaphore_signal(barrier, inc=1, device_id=peer, device_id_type=MESH)
    pl.semaphore_wait(barrier, len(peers))
    for d in (2, -2):
        pl.semaphore_signal(far1, inc=1, device_id=at_z(d), device_id_type=MESH)
    first.wait()

    started = []

    def send(src, dst, peer):
        i = len(started)
        copy = pltpu.make_async_remote_copy(
            src_ref=src, dst_ref=dst, send_sem=sends.at[i], recv_sem=recvs.at[i],
            device_id=peer, device_id_type=MESH,
        )
        copy.start()
        started.append(copy)
        return copy

    def arrived(copies):
        for copy in copies:
            copy.wait_recv()

    def panel_copy(owner, d):
        rows = at.at[pl.ds(pl.multiple_of(owner * PANEL, PANEL), PANEL)]
        return pltpu.make_async_remote_copy(
            src_ref=rows, dst_ref=rows, send_sem=p_send.at[d - 1], recv_sem=p_recv.at[owner],
            device_id=at_col(d), device_id_type=MESH,
        )

    @pl.when(col < PANELS)
    def _():
        at[pl.ds(pl.multiple_of(col * PANEL, PANEL), PANEL), :] = slab[:, 0:128].T[:PANEL]
        for d in (4, 3, 5, 2, 6, 7, 1):
            panel_copy(col, d).start()

    pl.semaphore_wait(far1, 2)
    for d in (4, -4):
        pl.semaphore_signal(far2, inc=1, device_id=at_z(d), device_id_type=MESH)
    rest.wait()
    for k in range(PANELS):
        @pl.when(col != k)
        def _():
            panel_copy(k, 1).wait_recv()

    panels_t = at[...]

    gp[0:24] = dot_t(panels_t, panels_t[0:128]).reshape(24, 8, 128)
    gp[24:32] = dot_t(panels_t[128:192], jnp.concatenate([panels_t[128:192], panels_t[128:192]], 0)).reshape(8, 8, 128)
    mine = 4 * col + x
    c_g1 = [send(gp.at[4 * col + (x + d) % 4], g1.at[d - 1], at_x(d)) for d in (2, 1, 3)]

    def around_z(piece, half_a, half_b, dst, dst_a, dst_b):
        far = (zlo + 2) % 4
        return [
            send(half_a(far), dst_a, at_z(2)),
            send(half_b(far), dst_b, at_z(-2)),
            send(piece((zlo + 1) % 4), dst[0], at_z(1)),
            send(piece((zlo + 3) % 4), dst[1], at_z(-1)),
        ]

    def rows48(i):
        return pl.ds(pl.multiple_of(48 * i, 8), 48)

    def rows24(i, half):
        return pl.ds(pl.multiple_of(48 * i + 24 * half, 8), 24)

    def x_products(h):
        m = dot(panels_t, slab[:, 512 * h:512 * h + 512])
        for q in range(4):
            mx[h, q] = m[:, 128 * q:128 * q + 128]

    def z_products(h):
        mz[h] = dot(panels_t, slab[:, 1024 + 512 * h:1536 + 512 * h])

    def x1(h):
        return [send(mx.at[h, (x + d) % 4], rx1.at[h, d - 1], at_x(d)) for d in (2, 1, 3)]

    def z1(h):
        return around_z(
            lambda i: mz.at[h, rows48(i)], lambda i: mz.at[h, rows24(i, 0)], lambda i: mz.at[h, rows24(i, 1)],
            (rz1a.at[h], rz1b.at[h]), rz1c.at[h, 0:24], rz1c.at[h, 24:48],
        )

    def x2(h, before):
        arrived(before)
        px[h] = mx[h, x] + rx1[h, 0] + rx1[h, 1] + rx1[h, 2]
        return around_z(
            lambda i: px.at[h, rows48(i)], lambda i: px.at[h, rows24(i, 0)], lambda i: px.at[h, rows24(i, 1)],
            (rx2a.at[h], rx2b.at[h]), rx2c.at[h, 0:24], rx2c.at[h, 24:48],
        )

    def z2(h, before):
        arrived(before)
        for q in range(4):
            cols = slice(128 * q, 128 * q + 128)
            pz[h, q] = mz[h, rows48(zlo), cols] + rz1a[h, :, cols] + rz1b[h, :, cols] + rz1c[h, :, cols]
        return [send(pz.at[h, (x + d) % 4], rz2.at[h, d - 1], at_x(d)) for d in (2, 1, 3)]

    def across_z(s):
        return [send(rr.at[s, zhi], rr.at[s, zhi], at_z(4 * e)) for e in (2, 1, 3)]

    def x3(h, before):
        arrived(before)
        rr[h, zhi] = px[h, rows48(zlo), :] + rx2a[h] + rx2b[h] + rx2c[h]
        return across_z(h)

    def z3(h, before):
        arrived(before)
        rr[2 + h, zhi] = pz[h, x] + rz2[h, 0] + rz2[h, 1] + rz2[h, 2]
        return across_z(2 + h)

    def own_rows(ref, at_rows):
        whole, half_a, half_b = (at_rows(ref, rows) for rows in (rows48(zlo), rows24(zlo, 0), rows24(zlo, 1)))
        return around_z(
            lambda i: whole, lambda i: half_a, lambda i: half_b, (whole, whole), half_a, half_b
        )

    def x4(h, before):
        arrived(before)
        mfx[h, x, rows48(zlo), :] = rr[h, 0] + rr[h, 1] + rr[h, 2] + rr[h, 3]
        return own_rows(mfx.at[h, x], lambda ref, rows: ref.at[rows])

    def z4(h, before):
        arrived(before)
        mfz[h, x, rows48(zlo), :] = rr[2 + h, 0] + rr[2 + h, 1] + rr[2 + h, 2] + rr[2 + h, 3]
        own = mfz.at[h, x, rows48(zlo)]
        return [send(own, own, at_x(d)) for d in (2, 1, 3)]

    def z5(h, before):
        arrived(before)
        return own_rows(mfz.at[h], lambda ref, rows: ref.at[:, rows])

    z_products(0)
    c_z1 = [z1(0)]
    x_products(0)
    c_x1 = [x1(0)]
    x_products(1)
    c_x1.append(x1(1))
    z_products(1)
    arrived(c_g1)
    g2[z] = gp[mine] + g1[0] + g1[1] + g1[2]
    pl.semaphore_wait(far2, 2)
    c_g2 = [send(g2.at[z], g2.at[z], at_z(d)) for d in (8, 7, 9, 6, 10, 5, 11, 4, 12, 3, 13, 2, 14, 1, 15)]
    c_z1.append(z1(1))

    c_z2 = [z2(0, c_z1[0])]
    c_x2 = [x2(0, c_x1[0])]
    c_x2.append(x2(1, c_x1[1]))
    arrived(c_g2)
    total = g2[0]
    for i in range(1, 16):
        total = total + g2[i]
    gfull[mine] = total
    c_g4 = [send(gfull.at[mine], gfull.at[mine], at_x(d)) for d in (2, 1, 3)]
    c_z3 = [z3(0, c_z2[0])]
    c_z2.append(z2(1, c_z1[1]))
    c_x3 = [x3(0, c_x2[0])]
    arrived(c_g4)
    four = gfull.at[pl.ds(4 * col, 4)]
    c_g5 = [send(four, four, at_col(d)) for d in (4, 3, 5, 2, 6, 7, 1)]
    c_x3.append(x3(1, c_x2[1]))
    c_z3.append(z3(1, c_z2[1]))
    arrived(c_g5)

    def block(i, j):
        if j == 2:
            return gfull[24:32].reshape(64, 128)[:, 0:64]
        return gfull[8 * i:8 * i + 8].reshape(64, 128)[:, 64 * j:64 * j + 64]

    t_ref[...] = jnp.zeros_like(t_ref)
    s_ref[...] = block(0, 0)
    t00 = eliminate(s_ref)
    l10, l20 = dot_t(block(1, 0), t00), dot_t(block(2, 0), t00)
    t_ref[0:64, 0:64] = t00
    l_ref[0], l_ref[1] = l10, l20
    s_ref[...] = block(1, 1) - dot_t(l10, l10)
    l_ref[2] = block(2, 1) - dot_t(l20, l10)
    l_ref[3] = block(2, 2) - dot_t(l20, l20)

    c_z4 = [z4(0, c_z3[0])]

    t11 = eliminate(s_ref)
    t_ref[64:128, 64:128] = t11
    l21 = dot_t(l_ref[2], t11)
    l_ref[2] = l21
    s_ref[...] = l_ref[3] - dot_t(l21, l21)

    c_x4 = [x4(0, c_x3[0])]

    t_ref[128:192, 128:192] = eliminate(s_ref)

    c_x4.append(x4(1, c_x3[1]))
    c_z4.append(z4(1, c_z3[1]))
    c_z5 = [z5(0, c_z4[0])]
    arrived(c_x4[0])
    c_x5 = [[send(mfx.at[0, x], mfx.at[0, x], at_x(d)) for d in (2, 1, 3)]]

    t00, t11, t22 = (t_ref[i:i + 64, i:i + 64] for i in (0, 64, 128))
    l10, l20, l21 = l_ref[0], l_ref[1], l_ref[2]
    t10 = -dot(t11, dot(l10, t00))
    t_ref[64:128, 0:64] = t10
    t_ref[128:192, 0:64] = -dot(t22, dot(l20, t00) + dot(l21, t10))
    t_ref[128:192, 64:128] = -dot(t22, dot(l21, t11))
    q_ref[...] = dot(t_ref[...], at[...]).T

    norm_scale = 1.0 / math.sqrt(128 * 64)

    arrived(c_x4[1])
    cx[x] = dot(t_ref[...], mfx[1, x])
    c_x5.append([send(cx.at[x], cx.at[x], at_x(d)) for d in (2, 1, 3)])
    c_z5.append(z5(1, c_z4[1]))
    outs = []

    def finish(coeffs, first):
        i = len(outs) // 2
        cols = pl.ds(first, 256)
        r_buf[i] = coeffs * norm_scale
        outs.append(pltpu.make_async_copy(r_buf.at[i], r_out.at[:, cols], out_sem.at[2 * i]))
        outs[-1].start()
        u_buf[i] = slab[:, cols] - dot(q_ref[...], coeffs)
        outs.append(pltpu.make_async_copy(u_buf.at[i], u_out.at[:, cols], out_sem.at[2 * i + 1]))
        outs[-1].start()

    def finish_all(coeffs_of, chunks, first):
        for q in (0, 2):
            finish(coeffs_of(jnp.concatenate([chunks[q], chunks[q + 1]], 1)), first + 128 * q)

    def from_products(m):
        return dot(t_ref[...], m)

    arrived(c_z5[0])
    finish_all(from_products, [mfz[0, q] for q in range(4)], 1024)
    arrived(c_x5[0])
    finish_all(from_products, [mfx[0, q] for q in range(4)], 0)
    arrived(c_x5[1])
    finish_all(lambda coeffs: coeffs, [cx[q] for q in range(4)], 512)
    arrived(c_z5[1])
    finish_all(from_products, [mfz[1, q] for q in range(4)], 1536)

    for copy in outs:
        copy.wait()
    for copy in started:
        copy.wait_send()

    @pl.when(col < PANELS)
    def _():
        for d in range(1, 8):
            panel_copy(col, d).wait_send()


def write_out(r_in, u_in, r_out, u_out, sems):
    copies = [
        pltpu.make_async_copy(r_in, r_out, sems.at[0]),
        pltpu.make_async_copy(u_in, u_out, sems.at[1]),
    ]
    for copy in copies:
        copy.start()
    for copy in copies:
        copy.wait()


MESSAGES = 96


def on_device(slab):
    hbm = pl.BlockSpec(memory_space=pltpu.HBM)
    place = pl.BlockSpec(memory_space=pl.ANY)

    def buf(*shape):
        return pltpu.VMEM(shape, F32)

    results = pl.pallas_call(
        kernel,
        out_shape=(
            jax.ShapeDtypeStruct((N, 2048), F32),
            jax.ShapeDtypeStruct((128, 2048), F32),
        ),
        in_specs=[hbm],
        out_specs=(place, place),
        scratch_shapes=[
            buf(128, 2048), buf(8, N, 256), buf(8, 128, 256), buf(N, 128), buf(32, 8, 128), buf(3, 8, 128), buf(16, 8, 128), buf(32, 8, 128),
            buf(2, 4, N, 128), buf(2, N, 512), buf(2, 3, N, 128), buf(2, 48, 512), buf(2, 48, 512), buf(2, 48, 512),
            buf(2, N, 128), buf(2, 4, 48, 128), buf(2, 48, 128), buf(2, 48, 128), buf(2, 48, 128), buf(2, 3, 48, 128),
            buf(4, 4, 48, 128), buf(2, 4, N, 128), buf(2, 4, N, 128), buf(4, N, 128),
            buf(64, 64), buf(4, 64, 64), buf(N, N), buf(128, N),
            pltpu.SemaphoreType.DMA((7,)), pltpu.SemaphoreType.DMA((PANELS,)),
            pltpu.SemaphoreType.DMA((MESSAGES,)), pltpu.SemaphoreType.DMA((MESSAGES,)),
            pltpu.SemaphoreType.DMA((2,)), pltpu.SemaphoreType.DMA((16,)),
            pltpu.SemaphoreType.REGULAR, pltpu.SemaphoreType.REGULAR,
        ],
        compiler_params=pltpu.CompilerParams(
            collective_id=0, has_side_effects=True, vmem_limit_bytes=50 << 20
        ),
    )(slab)
    return pl.pallas_call(
        write_out,
        out_shape=(
            jax.ShapeDtypeStruct((N, 2048), F32),
            jax.ShapeDtypeStruct((128, 2048), F32),
        ),
        in_specs=[place, place],
        out_specs=(place, place),
        scratch_shapes=[pltpu.SemaphoreType.DMA((2,))],
        compiler_params=pltpu.CompilerParams(vmem_limit_bytes=8 << 20),
    )(*results)


def solution(mesh):
    return jax.shard_map(
        on_device,
        mesh=mesh,
        in_specs=(P("rows", "cols"),),
        out_specs=(P(None, "cols"), P("rows", "cols")),
        check_vma=False,
    )
```

```python
import functools
import math

import jax
import jax.numpy as jnp
from jax import lax
from jax.experimental import pallas as pl
from jax.experimental.pallas import tpu as pltpu
from jax.sharding import PartitionSpec as P

MESH = pl.DeviceIdType.MESH
PANEL = 64
PANELS = 3
N = PANEL * PANELS
F32 = jnp.float32


def dot(a, b, dims=((1,), (0,))):
    return lax.dot_general(
        a, b, (dims, ((), ())), precision=lax.Precision.HIGHEST, preferred_element_type=F32
    )


def dot_t(a, b):
    return dot(a, b, ((1,), (1,)))


def eliminate(s_ref, begin, end):
    n = PANEL
    lane = lax.broadcasted_iota(jnp.int32, (n, n), 1)
    sub = lax.broadcasted_iota(jnp.int32, (n, n), 0)
    row_lane = lax.broadcasted_iota(jnp.int32, (1, n), 1)
    col_sub = lax.broadcasted_iota(jnp.int32, (n, 1), 0)

    def pick(value, where):
        return jnp.sum(jnp.where(where, value, 0.0), axis=1, keepdims=True)

    def step(i, _):
        j = 2 * i
        s = s_ref[...]
        r0 = s_ref[pl.ds(j, 1), :]
        r1 = s_ref[pl.ds(j + 1, 1), :]
        a = pick(r0, row_lane == j)
        b = pick(r1, row_lane == j)
        d = pick(r1, row_lane == j + 1)
        c0 = pick(s, lane == j)
        c1 = pick(s, lane == j + 1)
        a_inv = 1.0 / a
        ratio = b * a_inv
        second = d - b * ratio
        second_inv = 1.0 / second
        r0m = jnp.where(row_lane == j, 1.0, r0)
        r1n = jnp.where(row_lane == j, 0.0, r1) - ratio * r0m
        r0u = jnp.where(row_lane == j + 1, 0.0, r0m) * a_inv
        r1u = jnp.where(row_lane == j + 1, 1.0, r1n) * second_inv
        r1s = jnp.where(row_lane == j + 1, second, r1n)
        below = col_sub > j + 1
        c0b = jnp.where(below, c0, 0.0)
        c1b = jnp.where(below, c1 - c0 * ratio, 0.0)
        base = jnp.where((lane >= j) & (lane <= j + 1) & (sub > j + 1), 0.0, s)
        s_ref[...] = jnp.where(sub == j + 1, r1s, base - c0b * r0u - c1b * r1u)
        return 0

    lax.fori_loop(begin // 2, end // 2, step, 0)


def inverse_factor(s_ref):
    lane = lax.broadcasted_iota(jnp.int32, (PANEL, PANEL), 1)
    sub = lax.broadcasted_iota(jnp.int32, (PANEL, PANEL), 0)
    s = s_ref[...]
    pivots = jnp.sum(jnp.where(lane == sub, s, 0.0), axis=1, keepdims=True)
    return jnp.where(lane < sub, s, jnp.where(lane == sub, 1.0, 0.0)) * (1.0 / jnp.sqrt(pivots))


def kernel(
    slab_hbm, r_out, u_out,
    slab, r_buf, u_buf, at, gp, g1, g2, gfull,
    mx, mz, rx1, rz1a, rz1b, rz1c, px, pz, rx2a, rx2b, rx2c, rz2, rr, mfx, mfz,
    s_ref, l_ref, t_ref, q_ref,
    p_send, p_recv, sends, recvs, in_sem, out_sem, far1, far2,
):
    row, col = lax.axis_index("rows"), lax.axis_index("cols")
    z, x = row // 4, row % 4
    zhi, zlo = z // 4, z % 4

    def at_z(dz):
        return (((z + dz + 16) % 16) * 4 + x, col)

    def at_x(d):
        return (z * 4 + (x + d) % 4, col)

    def at_col(d):
        return (row, (col + d) % 8)

    first = pltpu.make_async_copy(slab_hbm.at[:, 0:256], slab.at[:, 0:256], in_sem.at[0])
    rest = pltpu.make_async_copy(slab_hbm.at[:, 256:2048], slab.at[:, 256:2048], in_sem.at[1])
    first.start()
    rest.start()

    z_peers = (1, -1, 2, -2)
    peers = [at_z(d) for d in z_peers] + [at_x(d) for d in (1, 2, 3)] + [at_col(d) for d in range(1, 8)]
    barrier = pltpu.get_barrier_semaphore()
    for peer in peers:
        pl.semaphore_signal(barrier, inc=1, device_id=peer, device_id_type=MESH)
    pl.semaphore_wait(barrier, len(peers))
    for d in (2, -2):
        pl.semaphore_signal(far1, inc=1, device_id=at_z(d), device_id_type=MESH)
    first.wait()

    started = []

    def send(src, dst, peer):
        i = len(started)
        copy = pltpu.make_async_remote_copy(
            src_ref=src, dst_ref=dst, send_sem=sends.at[i], recv_sem=recvs.at[i],
            device_id=peer, device_id_type=MESH,
        )
        copy.start()
        started.append(copy)
        return copy

    def arrived(copies):
        for copy in copies:
            copy.wait_recv()

    def panel_copy(owner, d):
        rows = at.at[pl.ds(pl.multiple_of(owner * PANEL, PANEL), PANEL)]
        return pltpu.make_async_remote_copy(
            src_ref=rows, dst_ref=rows, send_sem=p_send.at[d - 1], recv_sem=p_recv.at[owner],
            device_id=at_col(d), device_id_type=MESH,
        )

    @pl.when(col < PANELS)
    def _():
        at[pl.ds(pl.multiple_of(col * PANEL, PANEL), PANEL), :] = slab[:, 0:128].T[:PANEL]
        for d in (4, 3, 5, 2, 6, 7, 1):
            panel_copy(col, d).start()

    pl.semaphore_wait(far1, 2)
    for d in (4, -4):
        pl.semaphore_signal(far2, inc=1, device_id=at_z(d), device_id_type=MESH)
    rest.wait()
    for k in range(PANELS):
        @pl.when(col != k)
        def _():
            panel_copy(k, 1).wait_recv()

    panels_t = at[...]

    gp[0:24] = dot_t(panels_t, panels_t[0:128]).reshape(24, 8, 128)
    gp[24:32] = dot_t(panels_t[128:192], jnp.concatenate([panels_t[128:192], panels_t[128:192]], 0)).reshape(8, 8, 128)
    mine = 4 * col + x
    c_g1 = [send(gp.at[4 * col + (x + d) % 4], g1.at[d - 1], at_x(d)) for d in (2, 1, 3)]

    def around_z(piece, half_a, half_b, dst, dst_a, dst_b):
        far = (zlo + 2) % 4
        return [
            send(half_a(far), dst_a, at_z(2)),
            send(half_b(far), dst_b, at_z(-2)),
            send(piece((zlo + 1) % 4), dst[0], at_z(1)),
            send(piece((zlo + 3) % 4), dst[1], at_z(-1)),
        ]

    def rows48(i):
        return pl.ds(pl.multiple_of(48 * i, 8), 48)

    def rows24(i, half):
        return pl.ds(pl.multiple_of(48 * i + 24 * half, 8), 24)

    def x_products(h):
        m = dot(panels_t, slab[:, 512 * h:512 * h + 512])
        for q in range(4):
            mx[h, q] = m[:, 128 * q:128 * q + 128]

    def z_products(h):
        mz[h] = dot(panels_t, slab[:, 1536:2048])

    def x1(h):
        return [send(mx.at[h, (x + d) % 4], rx1.at[h, d - 1], at_x(d)) for d in (2, 1, 3)]

    def z1(h):
        return around_z(
            lambda i: mz.at[h, rows48(i)], lambda i: mz.at[h, rows24(i, 0)], lambda i: mz.at[h, rows24(i, 1)],
            (rz1a.at[h], rz1b.at[h]), rz1c.at[h, 0:24], rz1c.at[h, 24:48],
        )

    def x2(h, before):
        arrived(before)
        px[h] = mx[h, x] + rx1[h, 0] + rx1[h, 1] + rx1[h, 2]
        return around_z(
            lambda i: px.at[h, rows48(i)], lambda i: px.at[h, rows24(i, 0)], lambda i: px.at[h, rows24(i, 1)],
            (rx2a.at[h], rx2b.at[h]), rx2c.at[h, 0:24], rx2c.at[h, 24:48],
        )

    def z2(h, before):
        arrived(before)
        for q in range(4):
            cols = slice(128 * q, 128 * q + 128)
            pz[h, q] = mz[h, rows48(zlo), cols] + rz1a[h, :, cols] + rz1b[h, :, cols] + rz1c[h, :, cols]
        return [send(pz.at[h, (x + d) % 4], rz2.at[h, d - 1], at_x(d)) for d in (2, 1, 3)]

    def across_z(s):
        return [send(rr.at[s, zhi], rr.at[s, zhi], at_z(4 * e)) for e in (2, 1, 3)]

    def x3(h, before):
        arrived(before)
        rr[h, zhi] = px[h, rows48(zlo), :] + rx2a[h] + rx2b[h] + rx2c[h]
        return across_z(h)

    def z3(h, before):
        arrived(before)
        rr[3 + h, zhi] = pz[h, x] + rz2[h, 0] + rz2[h, 1] + rz2[h, 2]
        return across_z(3 + h)

    def own_rows(ref, at_rows):
        whole, half_a, half_b = (at_rows(ref, rows) for rows in (rows48(zlo), rows24(zlo, 0), rows24(zlo, 1)))
        return around_z(
            lambda i: whole, lambda i: half_a, lambda i: half_b, (whole, whole), half_a, half_b
        )

    def x4(h, before):
        arrived(before)
        mfx[h, x, rows48(zlo), :] = rr[h, 0] + rr[h, 1] + rr[h, 2] + rr[h, 3]
        return own_rows(mfx.at[h, x], lambda ref, rows: ref.at[rows])

    def z4(h, before):
        arrived(before)
        mfz[h, x, rows48(zlo), :] = rr[3 + h, 0] + rr[3 + h, 1] + rr[3 + h, 2] + rr[3 + h, 3]
        own = mfz.at[h, x, rows48(zlo)]
        return [send(own, own, at_x(d)) for d in (2, 1, 3)]

    def z5(h, before):
        arrived(before)
        return own_rows(mfz.at[h], lambda ref, rows: ref.at[:, rows])

    z_products(0)
    c_z1 = z1(0)
    c_x1 = []
    for h in range(3):
        x_products(h)
        c_x1.append(x1(h))
    arrived(c_g1)
    g2[z] = gp[mine] + g1[0] + g1[1] + g1[2]
    pl.semaphore_wait(far2, 2)
    c_g2 = [send(g2.at[z], g2.at[z], at_z(d)) for d in (8, 7, 9, 6, 10, 5, 11, 4, 12, 3, 13, 2, 14, 1, 15)]

    c_z2 = z2(0, c_z1)
    c_x2 = [x2(0, c_x1[0])]
    c_x2.append(x2(1, c_x1[1]))
    arrived(c_g2)
    total = g2[0]
    for i in range(1, 16):
        total = total + g2[i]
    gfull[mine] = total
    c_g4 = [send(gfull.at[mine], gfull.at[mine], at_x(d)) for d in (2, 1, 3)]
    c_x3 = [x3(0, c_x2[0])]
    c_x2.append(x2(2, c_x1[2]))
    c_z3 = z3(0, c_z2)
    c_x3.append(x3(1, c_x2[1]))
    arrived(c_g4)
    four = gfull.at[pl.ds(4 * col, 4)]
    c_g5 = [send(four, four, at_col(d)) for d in (4, 3, 5, 2, 6, 7, 1)]
    c_x3.append(x3(2, c_x2[2]))
    arrived(c_g5)

    def x5(h, before):
        arrived(before)
        return [send(mfx.at[h, x], mfx.at[h, x], at_x(d)) for d in (2, 1, 3)]

    def block(i, j):
        if j == 2:
            return gfull[24:32].reshape(64, 128)[:, 0:64]
        return gfull[8 * i:8 * i + 8].reshape(64, 128)[:, 64 * j:64 * j + 64]

    t_ref[...] = jnp.zeros_like(t_ref)
    s_ref[...] = block(0, 0)
    eliminate(s_ref, 0, 32)

    c_x4 = [x4(0, c_x3[0])]

    eliminate(s_ref, 32, 64)
    t00 = inverse_factor(s_ref)
    l10, l20 = dot_t(block(1, 0), t00), dot_t(block(2, 0), t00)
    t_ref[0:64, 0:64] = t00
    l_ref[0], l_ref[1] = l10, l20
    s_ref[...] = block(1, 1) - dot_t(l10, l10)
    l_ref[2] = block(2, 1) - dot_t(l20, l10)
    l_ref[3] = block(2, 2) - dot_t(l20, l20)

    c_x4.append(x4(1, c_x3[1]))
    c_z4 = z4(0, c_z3)

    eliminate(s_ref, 0, 32)

    c_x5 = [x5(0, c_x4[0])]

    eliminate(s_ref, 32, 64)
    t11 = inverse_factor(s_ref)
    t_ref[64:128, 64:128] = t11
    l21 = dot_t(l_ref[2], t11)
    l_ref[2] = l21
    s_ref[...] = l_ref[3] - dot_t(l21, l21)

    c_x4.append(x4(2, c_x3[2]))
    c_x5.append(x5(1, c_x4[1]))
    c_z5 = z5(0, c_z4)

    eliminate(s_ref, 0, 64)
    t_ref[128:192, 128:192] = inverse_factor(s_ref)
    c_x5.append(x5(2, c_x4[2]))

    t00, t11, t22 = (t_ref[i:i + 64, i:i + 64] for i in (0, 64, 128))
    l10, l20, l21 = l_ref[0], l_ref[1], l_ref[2]
    t10 = -dot(t11, dot(l10, t00))
    t_ref[64:128, 0:64] = t10
    t_ref[128:192, 0:64] = -dot(t22, dot(l20, t00) + dot(l21, t10))
    t_ref[128:192, 64:128] = -dot(t22, dot(l21, t11))
    q_ref[...] = dot(t_ref[...], at[...]).T

    norm_scale = 1.0 / math.sqrt(128 * 64)

    outs = []

    def finish(coeffs, first):
        i = len(outs) // 2
        cols = pl.ds(first, 256)
        r_buf[i] = coeffs * norm_scale
        outs.append(pltpu.make_async_copy(r_buf.at[i], r_out.at[:, cols], out_sem.at[2 * i]))
        outs[-1].start()
        u_buf[i] = slab[:, cols] - dot(q_ref[...], coeffs)
        outs.append(pltpu.make_async_copy(u_buf.at[i], u_out.at[:, cols], out_sem.at[2 * i + 1]))
        outs[-1].start()

    def finish_all(before, products, first):
        arrived(before)
        for q in (0, 2):
            pair = jnp.concatenate([products[q], products[q + 1]], 1)
            finish(dot(t_ref[...], pair), first + 128 * q)

    finish_all(c_x5[0], mfx.at[0], 0)
    finish_all(c_z5, mfz.at[0], 1536)
    finish_all(c_x5[1], mfx.at[1], 512)
    finish_all(c_x5[2], mfx.at[2], 1024)

    for copy in outs:
        copy.wait()
    for copy in started:
        copy.wait_send()

    @pl.when(col < PANELS)
    def _():
        for d in range(1, 8):
            panel_copy(col, d).wait_send()


def write_out(r_in, u_in, r_out, u_out, sems):
    copies = [
        pltpu.make_async_copy(r_in, r_out, sems.at[0]),
        pltpu.make_async_copy(u_in, u_out, sems.at[1]),
    ]
    for copy in copies:
        copy.start()
    for copy in copies:
        copy.wait()


MESSAGES = 96


def on_device(slab):
    hbm = pl.BlockSpec(memory_space=pltpu.HBM)
    place = pl.BlockSpec(memory_space=pl.ANY)

    def buf(*shape):
        return pltpu.VMEM(shape, F32)

    results = pl.pallas_call(
        kernel,
        out_shape=(
            jax.ShapeDtypeStruct((N, 2048), F32),
            jax.ShapeDtypeStruct((128, 2048), F32),
        ),
        in_specs=[hbm],
        out_specs=(place, place),
        scratch_shapes=[
            buf(128, 2048), buf(8, N, 256), buf(8, 128, 256), buf(N, 128), buf(32, 8, 128), buf(3, 8, 128), buf(16, 8, 128), buf(32, 8, 128),
            buf(3, 4, N, 128), buf(1, N, 512), buf(3, 3, N, 128), buf(1, 48, 512), buf(1, 48, 512), buf(1, 48, 512),
            buf(3, N, 128), buf(1, 4, 48, 128), buf(3, 48, 128), buf(3, 48, 128), buf(3, 48, 128), buf(1, 3, 48, 128),
            buf(4, 4, 48, 128), buf(3, 4, N, 128), buf(1, 4, N, 128),
            buf(64, 64), buf(4, 64, 64), buf(N, N), buf(128, N),
            pltpu.SemaphoreType.DMA((7,)), pltpu.SemaphoreType.DMA((PANELS,)),
            pltpu.SemaphoreType.DMA((MESSAGES,)), pltpu.SemaphoreType.DMA((MESSAGES,)),
            pltpu.SemaphoreType.DMA((2,)), pltpu.SemaphoreType.DMA((16,)),
            pltpu.SemaphoreType.REGULAR, pltpu.SemaphoreType.REGULAR,
        ],
        compiler_params=pltpu.CompilerParams(
            collective_id=0, has_side_effects=True, vmem_limit_bytes=50 << 20
        ),
    )(slab)
    return pl.pallas_call(
        write_out,
        out_shape=(
            jax.ShapeDtypeStruct((N, 2048), F32),
            jax.ShapeDtypeStruct((128, 2048), F32),
        ),
        in_specs=[place, place],
        out_specs=(place, place),
        scratch_shapes=[pltpu.SemaphoreType.DMA((2,))],
        compiler_params=pltpu.CompilerParams(vmem_limit_bytes=8 << 20),
    )(*results)


def solution(mesh):
    return jax.shard_map(
        on_device,
        mesh=mesh,
        in_specs=(P("rows", "cols"),),
        out_specs=(P(None, "cols"), P("rows", "cols")),
        check_vma=False,
    )
```

```python
import functools
import math

import jax
import jax.numpy as jnp
from jax import lax
from jax.experimental import pallas as pl
from jax.experimental.pallas import tpu as pltpu
from jax.sharding import PartitionSpec as P

MESH = pl.DeviceIdType.MESH
PANEL = 64
PANELS = 3
N = PANEL * PANELS
F32 = jnp.float32


def dot(a, b, dims=((1,), (0,))):
    return lax.dot_general(
        a, b, (dims, ((), ())), precision=lax.Precision.HIGHEST, preferred_element_type=F32
    )


def dot_t(a, b):
    return dot(a, b, ((1,), (1,)))


def eliminate(s_ref, begin, end):
    n = PANEL
    lane = lax.broadcasted_iota(jnp.int32, (n, n), 1)
    sub = lax.broadcasted_iota(jnp.int32, (n, n), 0)
    row_lane = lax.broadcasted_iota(jnp.int32, (1, n), 1)
    col_sub = lax.broadcasted_iota(jnp.int32, (n, 1), 0)

    def pick(value, where):
        return jnp.sum(jnp.where(where, value, 0.0), axis=1, keepdims=True)

    def step(i, _):
        j = 2 * i
        s = s_ref[...]
        r0 = s_ref[pl.ds(j, 1), :]
        r1 = s_ref[pl.ds(j + 1, 1), :]
        a = pick(r0, row_lane == j)
        b = pick(r1, row_lane == j)
        d = pick(r1, row_lane == j + 1)
        c0 = pick(s, lane == j)
        c1 = pick(s, lane == j + 1)
        a_inv = 1.0 / a
        ratio = b * a_inv
        second = d - b * ratio
        second_inv = 1.0 / second
        r0m = jnp.where(row_lane == j, 1.0, r0)
        r1n = jnp.where(row_lane == j, 0.0, r1) - ratio * r0m
        r0u = jnp.where(row_lane == j + 1, 0.0, r0m) * a_inv
        r1u = jnp.where(row_lane == j + 1, 1.0, r1n) * second_inv
        r1s = jnp.where(row_lane == j + 1, second, r1n)
        below = col_sub > j + 1
        c0b = jnp.where(below, c0, 0.0)
        c1b = jnp.where(below, c1 - c0 * ratio, 0.0)
        base = jnp.where((lane >= j) & (lane <= j + 1) & (sub > j + 1), 0.0, s)
        s_ref[...] = jnp.where(sub == j + 1, r1s, base - c0b * r0u - c1b * r1u)
        return 0

    lax.fori_loop(begin // 2, end // 2, step, 0)


def inverse_factor(s_ref):
    lane = lax.broadcasted_iota(jnp.int32, (PANEL, PANEL), 1)
    sub = lax.broadcasted_iota(jnp.int32, (PANEL, PANEL), 0)
    s = s_ref[...]
    pivots = jnp.sum(jnp.where(lane == sub, s, 0.0), axis=1, keepdims=True)
    return jnp.where(lane < sub, s, jnp.where(lane == sub, 1.0, 0.0)) * (1.0 / jnp.sqrt(pivots))


def kernel(
    slab_hbm, r_out, u_out,
    slab, r_buf, u_buf, at, gp, g1, g2, gfull,
    mx, mz, rx1, rz1a, rz1b, rz1c, px, pz, rx2a, rx2b, rx2c, rz2, rr, mfx, mfz,
    s_ref, l_ref, t_ref, q_ref,
    p_send, p_recv, sends, recvs, in_sem, out_sem, far1, far2,
):
    row, col = lax.axis_index("rows"), lax.axis_index("cols")
    z, x = row // 4, row % 4
    zhi, zlo = z // 4, z % 4

    def at_z(dz):
        return (((z + dz + 16) % 16) * 4 + x, col)

    def at_x(d):
        return (z * 4 + (x + d) % 4, col)

    def at_col(d):
        return (row, (col + d) % 8)

    first = pltpu.make_async_copy(slab_hbm.at[:, 0:256], slab.at[:, 0:256], in_sem.at[0])
    rest = pltpu.make_async_copy(slab_hbm.at[:, 256:2048], slab.at[:, 256:2048], in_sem.at[1])
    first.start()
    rest.start()

    z_peers = (1, -1, 2, -2)
    peers = [at_z(d) for d in z_peers] + [at_x(d) for d in (1, 2, 3)] + [at_col(d) for d in range(1, 8)]
    barrier = pltpu.get_barrier_semaphore()
    for peer in peers:
        pl.semaphore_signal(barrier, inc=1, device_id=peer, device_id_type=MESH)
    pl.semaphore_wait(barrier, len(peers))
    for d in (2, -2):
        pl.semaphore_signal(far1, inc=1, device_id=at_z(d), device_id_type=MESH)
    first.wait()

    started = []

    def send(src, dst, peer):
        i = len(started)
        copy = pltpu.make_async_remote_copy(
            src_ref=src, dst_ref=dst, send_sem=sends.at[i], recv_sem=recvs.at[i],
            device_id=peer, device_id_type=MESH,
        )
        copy.start()
        started.append(copy)
        return copy

    def arrived(copies):
        for copy in copies:
            copy.wait_recv()

    def panel_copy(owner, d):
        rows = at.at[pl.ds(pl.multiple_of(owner * PANEL, PANEL), PANEL)]
        return pltpu.make_async_remote_copy(
            src_ref=rows, dst_ref=rows, send_sem=p_send.at[d - 1], recv_sem=p_recv.at[owner],
            device_id=at_col(d), device_id_type=MESH,
        )

    @pl.when(col < PANELS)
    def _():
        at[pl.ds(pl.multiple_of(col * PANEL, PANEL), PANEL), :] = slab[:, 0:128].T[:PANEL]
        for d in (4, 3, 5, 2, 6, 7, 1):
            panel_copy(col, d).start()

    pl.semaphore_wait(far1, 2)
    for d in (4, -4):
        pl.semaphore_signal(far2, inc=1, device_id=at_z(d), device_id_type=MESH)
    rest.wait()
    for k in range(PANELS):
        @pl.when(col != k)
        def _():
            panel_copy(k, 1).wait_recv()

    panels_t = at[...]

    gp[0:24] = dot_t(panels_t, panels_t[0:128]).reshape(24, 8, 128)
    gp[24:32] = dot_t(panels_t[128:192], jnp.concatenate([panels_t[128:192], panels_t[128:192]], 0)).reshape(8, 8, 128)
    mine = 4 * col + x
    c_g1 = [send(gp.at[4 * col + (x + d) % 4], g1.at[d - 1], at_x(d)) for d in (2, 1, 3)]

    def around_z(piece, half_a, half_b, dst, dst_a, dst_b):
        far = (zlo + 2) % 4
        return [
            send(half_a(far), dst_a, at_z(2)),
            send(half_b(far), dst_b, at_z(-2)),
            send(piece((zlo + 1) % 4), dst[0], at_z(1)),
            send(piece((zlo + 3) % 4), dst[1], at_z(-1)),
        ]

    def rows48(i):
        return pl.ds(pl.multiple_of(48 * i, 8), 48)

    def rows24(i, half):
        return pl.ds(pl.multiple_of(48 * i + 24 * half, 8), 24)

    def x_products(h):
        m = dot(panels_t, slab[:, 512 * h:512 * h + 512])
        for q in range(4):
            mx[h, q] = m[:, 128 * q:128 * q + 128]

    def z_products(h):
        mz[h] = dot(panels_t, slab[:, 1024 + 512 * h:1536 + 512 * h])

    def x1(h):
        return [send(mx.at[h, (x + d) % 4], rx1.at[h, d - 1], at_x(d)) for d in (2, 1, 3)]

    def z1(h):
        return around_z(
            lambda i: mz.at[h, rows48(i)], lambda i: mz.at[h, rows24(i, 0)], lambda i: mz.at[h, rows24(i, 1)],
            (rz1a.at[h], rz1b.at[h]), rz1c.at[h, 0:24], rz1c.at[h, 24:48],
        )

    def x2(h, before):
        arrived(before)
        px[h] = mx[h, x] + rx1[h, 0] + rx1[h, 1] + rx1[h, 2]
        return around_z(
            lambda i: px.at[h, rows48(i)], lambda i: px.at[h, rows24(i, 0)], lambda i: px.at[h, rows24(i, 1)],
            (rx2a.at[h], rx2b.at[h]), rx2c.at[h, 0:24], rx2c.at[h, 24:48],
        )

    def z2(h, before):
        arrived(before)
        for q in range(4):
            cols = slice(128 * q, 128 * q + 128)
            pz[h, q] = mz[h, rows48(zlo), cols] + rz1a[h, :, cols] + rz1b[h, :, cols] + rz1c[h, :, cols]
        return [send(pz.at[h, (x + d) % 4], rz2.at[h, d - 1], at_x(d)) for d in (2, 1, 3)]

    def across_z(s):
        return [send(rr.at[s, zhi], rr.at[s, zhi], at_z(4 * e)) for e in (2, 1, 3)]

    def x3(h, before):
        arrived(before)
        rr[h, zhi] = px[h, rows48(zlo), :] + rx2a[h] + rx2b[h] + rx2c[h]
        return across_z(h)

    def z3(h, before):
        arrived(before)
        rr[2 + h, zhi] = pz[h, x] + rz2[h, 0] + rz2[h, 1] + rz2[h, 2]
        return across_z(2 + h)

    def own_rows(ref, at_rows):
        whole, half_a, half_b = (at_rows(ref, rows) for rows in (rows48(zlo), rows24(zlo, 0), rows24(zlo, 1)))
        return around_z(
            lambda i: whole, lambda i: half_a, lambda i: half_b, (whole, whole), half_a, half_b
        )

    def x4(h, before):
        arrived(before)
        mfx[h, x, rows48(zlo), :] = rr[h, 0] + rr[h, 1] + rr[h, 2] + rr[h, 3]
        return own_rows(mfx.at[h, x], lambda ref, rows: ref.at[rows])

    def z4(h, before):
        arrived(before)
        mfz[h, x, rows48(zlo), :] = rr[2 + h, 0] + rr[2 + h, 1] + rr[2 + h, 2] + rr[2 + h, 3]
        own = mfz.at[h, x, rows48(zlo)]
        return [send(own, own, at_x(d)) for d in (2, 1, 3)]

    def z5(h, before, chunks):
        arrived(before)
        return own_rows(mfz.at[h, chunks], lambda ref, rows: ref.at[:, rows])

    z_products(0)
    c_z1 = [z1(0)]
    c_x1 = []
    for h in range(2):
        x_products(h)
        c_x1.append(x1(h))
    z_products(1)
    arrived(c_g1)
    g2[z] = gp[mine] + g1[0] + g1[1] + g1[2]
    pl.semaphore_wait(far2, 2)
    c_g2 = [send(g2.at[z], g2.at[z], at_z(d)) for d in (8, 7, 9, 6, 10, 5, 11, 4, 12, 3, 13, 2, 14, 1, 15)]
    c_z1.append(z1(1))

    c_z2 = [z2(0, c_z1[0])]
    c_x2 = [x2(0, c_x1[0])]
    c_x2.append(x2(1, c_x1[1]))
    arrived(c_g2)
    total = g2[0]
    for i in range(1, 16):
        total = total + g2[i]
    gfull[mine] = total
    c_g4 = [send(gfull.at[mine], gfull.at[mine], at_x(d)) for d in (2, 1, 3)]
    c_z3 = [z3(0, c_z2[0])]
    c_z2.append(z2(1, c_z1[1]))
    c_x3 = [x3(0, c_x2[0])]
    arrived(c_g4)
    four = gfull.at[pl.ds(4 * col, 4)]
    c_g5 = [send(four, four, at_col(d)) for d in (4, 3, 5, 2, 6, 7, 1)]
    c_x3.append(x3(1, c_x2[1]))
    c_z3.append(z3(1, c_z2[1]))
    arrived(c_g5)

    def x5(h, before):
        arrived(before)
        return [send(mfx.at[h, x], mfx.at[h, x], at_x(d)) for d in (2, 1, 3)]

    def block(i, j):
        if j == 2:
            return gfull[24:32].reshape(64, 128)[:, 0:64]
        return gfull[8 * i:8 * i + 8].reshape(64, 128)[:, 64 * j:64 * j + 64]

    t_ref[...] = jnp.zeros_like(t_ref)
    s_ref[...] = block(0, 0)
    eliminate(s_ref, 0, 32)

    c_z4 = [z4(0, c_z3[0])]

    eliminate(s_ref, 32, 64)
    t00 = inverse_factor(s_ref)
    l10, l20 = dot_t(block(1, 0), t00), dot_t(block(2, 0), t00)
    t_ref[0:64, 0:64] = t00
    l_ref[0], l_ref[1] = l10, l20
    s_ref[...] = block(1, 1) - dot_t(l10, l10)
    l_ref[2] = block(2, 1) - dot_t(l20, l10)
    l_ref[3] = block(2, 2) - dot_t(l20, l20)

    c_x4 = [x4(0, c_x3[0])]

    eliminate(s_ref, 0, 32)

    c_x4.append(x4(1, c_x3[1]))
    c_z5 = [z5(0, c_z4[0], slice(0, 4))]

    eliminate(s_ref, 32, 64)
    t11 = inverse_factor(s_ref)
    t_ref[64:128, 64:128] = t11
    l21 = dot_t(l_ref[2], t11)
    l_ref[2] = l21
    s_ref[...] = l_ref[3] - dot_t(l21, l21)

    c_x5 = [x5(0, c_x4[0])]
    c_z4.append(z4(1, c_z3[1]))
    c_x5.append(x5(1, c_x4[1]))

    eliminate(s_ref, 0, 64)
    t_ref[128:192, 128:192] = inverse_factor(s_ref)
    c_z5.append(z5(1, c_z4[1], slice(0, 2)))
    c_z5.append(z5(1, [], slice(2, 4)))

    t00, t11, t22 = (t_ref[i:i + 64, i:i + 64] for i in (0, 64, 128))
    l10, l20, l21 = l_ref[0], l_ref[1], l_ref[2]
    t10 = -dot(t11, dot(l10, t00))
    t_ref[64:128, 0:64] = t10
    t_ref[128:192, 0:64] = -dot(t22, dot(l20, t00) + dot(l21, t10))
    t_ref[128:192, 64:128] = -dot(t22, dot(l21, t11))
    q_ref[...] = dot(t_ref[...], at[...]).T

    norm_scale = 1.0 / math.sqrt(128 * 64)

    outs = []

    def finish(coeffs, first):
        i = len(outs) // 2
        cols = pl.ds(first, 256)
        r_buf[i] = coeffs * norm_scale
        outs.append(pltpu.make_async_copy(r_buf.at[i], r_out.at[:, cols], out_sem.at[2 * i]))
        outs[-1].start()
        u_buf[i] = slab[:, cols] - dot(q_ref[...], coeffs)
        outs.append(pltpu.make_async_copy(u_buf.at[i], u_out.at[:, cols], out_sem.at[2 * i + 1]))
        outs[-1].start()

    def finish_pair(products, q, first):
        pair = jnp.concatenate([products[q], products[q + 1]], 1)
        finish(dot(t_ref[...], pair), first + 128 * q)

    for before, products, first in (
        (c_x5[0], mfx.at[0], 0), (c_z5[0], mfz.at[0], 1024), (c_x5[1], mfx.at[1], 512)
    ):
        arrived(before)
        for q in (0, 2):
            finish_pair(products, q, first)
    for q in (0, 2):
        arrived(c_z5[1 + q // 2])
        finish_pair(mfz.at[1], q, 1536)

    for copy in outs:
        copy.wait()
    for copy in started:
        copy.wait_send()

    @pl.when(col < PANELS)
    def _():
        for d in range(1, 8):
            panel_copy(col, d).wait_send()


def write_out(r_in, u_in, r_out, u_out, sems):
    copies = [
        pltpu.make_async_copy(r_in, r_out, sems.at[0]),
        pltpu.make_async_copy(u_in, u_out, sems.at[1]),
    ]
    for copy in copies:
        copy.start()
    for copy in copies:
        copy.wait()


MESSAGES = 100


def on_device(slab):
    hbm = pl.BlockSpec(memory_space=pltpu.HBM)
    place = pl.BlockSpec(memory_space=pl.ANY)

    def buf(*shape):
        return pltpu.VMEM(shape, F32)

    results = pl.pallas_call(
        kernel,
        out_shape=(
            jax.ShapeDtypeStruct((N, 2048), F32),
            jax.ShapeDtypeStruct((128, 2048), F32),
        ),
        in_specs=[hbm],
        out_specs=(place, place),
        scratch_shapes=[
            buf(128, 2048), buf(8, N, 256), buf(8, 128, 256), buf(N, 128), buf(32, 8, 128), buf(3, 8, 128), buf(16, 8, 128), buf(32, 8, 128),
            buf(2, 4, N, 128), buf(2, N, 512), buf(2, 3, N, 128), buf(2, 48, 512), buf(2, 48, 512), buf(2, 48, 512),
            buf(2, N, 128), buf(2, 4, 48, 128), buf(2, 48, 128), buf(2, 48, 128), buf(2, 48, 128), buf(2, 3, 48, 128),
            buf(4, 4, 48, 128), buf(2, 4, N, 128), buf(2, 4, N, 128),
            buf(64, 64), buf(4, 64, 64), buf(N, N), buf(128, N),
            pltpu.SemaphoreType.DMA((7,)), pltpu.SemaphoreType.DMA((PANELS,)),
            pltpu.SemaphoreType.DMA((MESSAGES,)), pltpu.SemaphoreType.DMA((MESSAGES,)),
            pltpu.SemaphoreType.DMA((2,)), pltpu.SemaphoreType.DMA((16,)),
            pltpu.SemaphoreType.REGULAR, pltpu.SemaphoreType.REGULAR,
        ],
        compiler_params=pltpu.CompilerParams(
            collective_id=0, has_side_effects=True, vmem_limit_bytes=50 << 20
        ),
    )(slab)
    return pl.pallas_call(
        write_out,
        out_shape=(
            jax.ShapeDtypeStruct((N, 2048), F32),
            jax.ShapeDtypeStruct((128, 2048), F32),
        ),
        in_specs=[place, place],
        out_specs=(place, place),
        scratch_shapes=[pltpu.SemaphoreType.DMA((2,))],
        compiler_params=pltpu.CompilerParams(vmem_limit_bytes=8 << 20),
    )(*results)


def solution(mesh):
    return jax.shard_map(
        on_device,
        mesh=mesh,
        in_specs=(P("rows", "cols"),),
        out_specs=(P(None, "cols"), P("rows", "cols")),
        check_vma=False,
    )
```

```python
import functools
import math

import jax
import jax.numpy as jnp
from jax import lax
from jax.experimental import pallas as pl
from jax.experimental.pallas import tpu as pltpu
from jax.sharding import PartitionSpec as P

MESH = pl.DeviceIdType.MESH
PANEL = 64
PANELS = 3
N = PANEL * PANELS
F32 = jnp.float32


def dot(a, b, dims=((1,), (0,))):
    return lax.dot_general(
        a, b, (dims, ((), ())), precision=lax.Precision.HIGHEST, preferred_element_type=F32
    )


def dot_t(a, b):
    return dot(a, b, ((1,), (1,)))


def eliminate(s_ref, begin, end):
    n = PANEL
    lane = lax.broadcasted_iota(jnp.int32, (n, n), 1)
    sub = lax.broadcasted_iota(jnp.int32, (n, n), 0)
    row_lane = lax.broadcasted_iota(jnp.int32, (1, n), 1)
    col_sub = lax.broadcasted_iota(jnp.int32, (n, 1), 0)

    def pick(value, where):
        return jnp.sum(jnp.where(where, value, 0.0), axis=1, keepdims=True)

    def step(i, _):
        j = 2 * i
        s = s_ref[...]
        r0 = s_ref[pl.ds(j, 1), :]
        r1 = s_ref[pl.ds(j + 1, 1), :]
        a = pick(r0, row_lane == j)
        b = pick(r1, row_lane == j)
        d = pick(r1, row_lane == j + 1)
        c0 = pick(s, lane == j)
        c1 = pick(s, lane == j + 1)
        a_inv = 1.0 / a
        ratio = b * a_inv
        second = d - b * ratio
        second_inv = 1.0 / second
        r0m = jnp.where(row_lane == j, 1.0, r0)
        r1n = jnp.where(row_lane == j, 0.0, r1) - ratio * r0m
        r0u = jnp.where(row_lane == j + 1, 0.0, r0m) * a_inv
        r1u = jnp.where(row_lane == j + 1, 1.0, r1n) * second_inv
        r1s = jnp.where(row_lane == j + 1, second, r1n)
        below = col_sub > j + 1
        c0b = jnp.where(below, c0, 0.0)
        c1b = jnp.where(below, c1 - c0 * ratio, 0.0)
        base = jnp.where((lane >= j) & (lane <= j + 1) & (sub > j + 1), 0.0, s)
        s_ref[...] = jnp.where(sub == j + 1, r1s, base - c0b * r0u - c1b * r1u)
        return 0

    lax.fori_loop(begin // 2, end // 2, step, 0)


def inverse_factor(s_ref):
    lane = lax.broadcasted_iota(jnp.int32, (PANEL, PANEL), 1)
    sub = lax.broadcasted_iota(jnp.int32, (PANEL, PANEL), 0)
    s = s_ref[...]
    pivots = jnp.sum(jnp.where(lane == sub, s, 0.0), axis=1, keepdims=True)
    return jnp.where(lane < sub, s, jnp.where(lane == sub, 1.0, 0.0)) * (1.0 / jnp.sqrt(pivots))


def kernel(
    slab_hbm, r_out, u_out,
    slab, r_buf, u_buf, at, gp, g1, g2, gfull,
    mx, mz, rx1, rz1a, rz1b, rz1c, px, pz, rx2a, rx2b, rx2c, rz2, rr, mfx, mfz,
    s_ref, l_ref, t_ref, q_ref,
    p_send, p_recv, sends, recvs, in_sem, out_sem, far1, far2,
):
    row, col = lax.axis_index("rows"), lax.axis_index("cols")
    z, x = row // 4, row % 4
    zhi, zlo = z // 4, z % 4

    def at_z(dz):
        return (((z + dz + 16) % 16) * 4 + x, col)

    def at_x(d):
        return (z * 4 + (x + d) % 4, col)

    def at_col(d):
        return (row, (col + d) % 8)

    first = pltpu.make_async_copy(slab_hbm.at[:, 0:256], slab.at[:, 0:256], in_sem.at[0])
    rest = pltpu.make_async_copy(slab_hbm.at[:, 256:2048], slab.at[:, 256:2048], in_sem.at[1])
    first.start()
    rest.start()

    z_peers = (1, -1, 2, -2)
    peers = [at_z(d) for d in z_peers] + [at_x(d) for d in (1, 2, 3)] + [at_col(d) for d in range(1, 8)]
    barrier = pltpu.get_barrier_semaphore()
    for peer in peers:
        pl.semaphore_signal(barrier, inc=1, device_id=peer, device_id_type=MESH)
    pl.semaphore_wait(barrier, len(peers))
    for d in (2, -2):
        pl.semaphore_signal(far1, inc=1, device_id=at_z(d), device_id_type=MESH)
    first.wait()

    started = []

    def send(src, dst, peer):
        i = len(started)
        copy = pltpu.make_async_remote_copy(
            src_ref=src, dst_ref=dst, send_sem=sends.at[i], recv_sem=recvs.at[i],
            device_id=peer, device_id_type=MESH,
        )
        copy.start()
        started.append(copy)
        return copy

    def arrived(copies):
        for copy in copies:
            copy.wait_recv()

    def panel_copy(owner, d):
        rows = at.at[pl.ds(pl.multiple_of(owner * PANEL, PANEL), PANEL)]
        return pltpu.make_async_remote_copy(
            src_ref=rows, dst_ref=rows, send_sem=p_send.at[d - 1], recv_sem=p_recv.at[owner],
            device_id=at_col(d), device_id_type=MESH,
        )

    @pl.when(col < PANELS)
    def _():
        at[pl.ds(pl.multiple_of(col * PANEL, PANEL), PANEL), :] = slab[:, 0:128].T[:PANEL]
        for d in (4, 3, 5, 2, 6, 7, 1):
            panel_copy(col, d).start()

    pl.semaphore_wait(far1, 2)
    for d in (4, -4):
        pl.semaphore_signal(far2, inc=1, device_id=at_z(d), device_id_type=MESH)
    rest.wait()
    for k in range(PANELS):
        @pl.when(col != k)
        def _():
            panel_copy(k, 1).wait_recv()

    panels_t = at[...]

    gp[0:24] = dot_t(panels_t, panels_t[0:128]).reshape(24, 8, 128)
    gp[24:32] = dot_t(panels_t[128:192], jnp.concatenate([panels_t[128:192], panels_t[128:192]], 0)).reshape(8, 8, 128)
    mine = 4 * col + x
    c_g1 = [send(gp.at[4 * col + (x + d) % 4], g1.at[d - 1], at_x(d)) for d in (2, 1, 3)]

    def around_z(piece, half_a, half_b, dst, dst_a, dst_b):
        far = (zlo + 2) % 4
        return [
            send(half_a(far), dst_a, at_z(2)),
            send(half_b(far), dst_b, at_z(-2)),
            send(piece((zlo + 1) % 4), dst[0], at_z(1)),
            send(piece((zlo + 3) % 4), dst[1], at_z(-1)),
        ]

    def rows48(i):
        return pl.ds(pl.multiple_of(48 * i, 8), 48)

    def rows24(i, half):
        return pl.ds(pl.multiple_of(48 * i + 24 * half, 8), 24)

    def x_products(h):
        m = dot(panels_t, slab[:, 512 * h:512 * h + 512])
        for q in range(4):
            mx[h, q] = m[:, 128 * q:128 * q + 128]

    def z_products(h):
        mz[h] = dot(panels_t, slab[:, 1024 + 512 * h:1536 + 512 * h])

    def x1(h):
        return [send(mx.at[h, (x + d) % 4], rx1.at[h, d - 1], at_x(d)) for d in (2, 1, 3)]

    def z1(h):
        return around_z(
            lambda i: mz.at[h, rows48(i)], lambda i: mz.at[h, rows24(i, 0)], lambda i: mz.at[h, rows24(i, 1)],
            (rz1a.at[h], rz1b.at[h]), rz1c.at[h, 0:24], rz1c.at[h, 24:48],
        )

    def x2(h, before):
        arrived(before)
        px[h] = mx[h, x] + rx1[h, 0] + rx1[h, 1] + rx1[h, 2]
        return around_z(
            lambda i: px.at[h, rows48(i)], lambda i: px.at[h, rows24(i, 0)], lambda i: px.at[h, rows24(i, 1)],
            (rx2a.at[h], rx2b.at[h]), rx2c.at[h, 0:24], rx2c.at[h, 24:48],
        )

    def z2(h, before):
        arrived(before)
        for q in range(4):
            cols = slice(128 * q, 128 * q + 128)
            pz[h, q] = mz[h, rows48(zlo), cols] + rz1a[h, :, cols] + rz1b[h, :, cols] + rz1c[h, :, cols]
        return [send(pz.at[h, (x + d) % 4], rz2.at[h, d - 1], at_x(d)) for d in (2, 1, 3)]

    def across_z(s):
        return [send(rr.at[s, zhi], rr.at[s, zhi], at_z(4 * e)) for e in (2, 1, 3)]

    def x3(h, before):
        arrived(before)
        rr[h, zhi] = px[h, rows48(zlo), :] + rx2a[h] + rx2b[h] + rx2c[h]
        return across_z(h)

    def z3(h, before):
        arrived(before)
        rr[2 + h, zhi] = pz[h, x] + rz2[h, 0] + rz2[h, 1] + rz2[h, 2]
        return across_z(2 + h)

    def own_rows(ref, at_rows):
        whole, half_a, half_b = (at_rows(ref, rows) for rows in (rows48(zlo), rows24(zlo, 0), rows24(zlo, 1)))
        return around_z(
            lambda i: whole, lambda i: half_a, lambda i: half_b, (whole, whole), half_a, half_b
        )

    def x4(h, before):
        arrived(before)
        mfx[h, x, rows48(zlo), :] = rr[h, 0] + rr[h, 1] + rr[h, 2] + rr[h, 3]
        return own_rows(mfx.at[h, x], lambda ref, rows: ref.at[rows])

    def z4(h, before):
        arrived(before)
        mfz[h, x, rows48(zlo), :] = rr[2 + h, 0] + rr[2 + h, 1] + rr[2 + h, 2] + rr[2 + h, 3]
        own = mfz.at[h, x, rows48(zlo)]
        return [send(own, own, at_x(d)) for d in (2, 1, 3)]

    def z5(h, before, chunks):
        arrived(before)
        return own_rows(mfz.at[h, chunks], lambda ref, rows: ref.at[:, rows])

    x_products(0)
    c_x1 = [x1(0)]
    z_products(0)
    c_z1 = [z1(0)]
    x_products(1)
    c_x1.append(x1(1))
    z_products(1)
    arrived(c_g1)
    g2[z] = gp[mine] + g1[0] + g1[1] + g1[2]
    pl.semaphore_wait(far2, 2)
    c_g2 = [send(g2.at[z], g2.at[z], at_z(d)) for d in (8, 7, 9, 6, 10, 5, 11, 4, 12, 3, 13, 2, 14, 1, 15)]
    c_z1.append(z1(1))

    c_x2 = [x2(0, c_x1[0])]
    c_z2 = [z2(0, c_z1[0])]
    c_x2.append(x2(1, c_x1[1]))
    c_x3 = [x3(0, c_x2[0])]
    arrived(c_g2)
    total = g2[0]
    for i in range(1, 16):
        total = total + g2[i]
    gfull[mine] = total
    c_g4 = [send(gfull.at[mine], gfull.at[mine], at_x(d)) for d in (2, 1, 3)]
    c_z3 = [z3(0, c_z2[0])]
    c_z2.append(z2(1, c_z1[1]))
    c_x3.append(x3(1, c_x2[1]))
    arrived(c_g4)
    four = gfull.at[pl.ds(4 * col, 4)]
    c_g5 = [send(four, four, at_col(d)) for d in (4, 3, 5, 2, 6, 7, 1)]
    c_z3.append(z3(1, c_z2[1]))
    arrived(c_g5)

    def x5(h, before):
        arrived(before)
        return [send(mfx.at[h, x], mfx.at[h, x], at_x(d)) for d in (2, 1, 3)]

    def block(i, j):
        if j == 2:
            return gfull[24:32].reshape(64, 128)[:, 0:64]
        return gfull[8 * i:8 * i + 8].reshape(64, 128)[:, 64 * j:64 * j + 64]

    t_ref[...] = jnp.zeros_like(t_ref)
    s_ref[...] = block(0, 0)
    eliminate(s_ref, 0, 32)

    c_x4 = [x4(0, c_x3[0])]
    c_z4 = [z4(0, c_z3[0])]

    eliminate(s_ref, 32, 64)
    t00 = inverse_factor(s_ref)
    l10, l20 = dot_t(block(1, 0), t00), dot_t(block(2, 0), t00)
    t_ref[0:64, 0:64] = t00
    l_ref[0], l_ref[1] = l10, l20
    s_ref[...] = block(1, 1) - dot_t(l10, l10)
    l_ref[2] = block(2, 1) - dot_t(l20, l10)
    l_ref[3] = block(2, 2) - dot_t(l20, l20)

    c_x4.append(x4(1, c_x3[1]))
    c_x5 = [x5(0, c_x4[0])]
    c_z5 = [z5(0, c_z4[0], slice(0, 4))]

    eliminate(s_ref, 0, 32)

    c_z4.append(z4(1, c_z3[1]))

    eliminate(s_ref, 32, 64)
    t11 = inverse_factor(s_ref)
    t_ref[64:128, 64:128] = t11
    l21 = dot_t(l_ref[2], t11)
    l_ref[2] = l21
    s_ref[...] = l_ref[3] - dot_t(l21, l21)

    c_x5.append(x5(1, c_x4[1]))

    eliminate(s_ref, 0, 32)

    c_z5.append(z5(1, c_z4[1], slice(0, 2)))
    c_z5.append(z5(1, [], slice(2, 4)))

    eliminate(s_ref, 32, 64)
    t_ref[128:192, 128:192] = inverse_factor(s_ref)

    t00, t11, t22 = (t_ref[i:i + 64, i:i + 64] for i in (0, 64, 128))
    l10, l20, l21 = l_ref[0], l_ref[1], l_ref[2]
    t10 = -dot(t11, dot(l10, t00))
    t_ref[64:128, 0:64] = t10
    t_ref[128:192, 0:64] = -dot(t22, dot(l20, t00) + dot(l21, t10))
    t_ref[128:192, 64:128] = -dot(t22, dot(l21, t11))
    q_ref[...] = dot(t_ref[...], at[...]).T

    norm_scale = 1.0 / math.sqrt(128 * 64)

    outs = []

    def finish(coeffs, first):
        i = len(outs) // 2
        cols = pl.ds(first, 256)
        r_buf[i] = coeffs * norm_scale
        outs.append(pltpu.make_async_copy(r_buf.at[i], r_out.at[:, cols], out_sem.at[2 * i]))
        outs[-1].start()
        u_buf[i] = slab[:, cols] - dot(q_ref[...], coeffs)
        outs.append(pltpu.make_async_copy(u_buf.at[i], u_out.at[:, cols], out_sem.at[2 * i + 1]))
        outs[-1].start()

    def finish_pair(products, q, first):
        pair = jnp.concatenate([products[q], products[q + 1]], 1)
        finish(dot(t_ref[...], pair), first + 128 * q)

    for before, products, first in (
        (c_x5[0], mfx.at[0], 0), (c_z5[0], mfz.at[0], 1024), (c_x5[1], mfx.at[1], 512)
    ):
        arrived(before)
        for q in (0, 2):
            finish_pair(products, q, first)
    for q in (0, 2):
        arrived(c_z5[1 + q // 2])
        finish_pair(mfz.at[1], q, 1536)

    for copy in outs:
        copy.wait()
    for copy in started:
        copy.wait_send()

    @pl.when(col < PANELS)
    def _():
        for d in range(1, 8):
            panel_copy(col, d).wait_send()


def write_out(r_in, u_in, r_out, u_out, sems):
    copies = [
        pltpu.make_async_copy(r_in, r_out, sems.at[0]),
        pltpu.make_async_copy(u_in, u_out, sems.at[1]),
    ]
    for copy in copies:
        copy.start()
    for copy in copies:
        copy.wait()


MESSAGES = 100


def on_device(slab):
    hbm = pl.BlockSpec(memory_space=pltpu.HBM)
    place = pl.BlockSpec(memory_space=pl.ANY)

    def buf(*shape):
        return pltpu.VMEM(shape, F32)

    results = pl.pallas_call(
        kernel,
        out_shape=(
            jax.ShapeDtypeStruct((N, 2048), F32),
            jax.ShapeDtypeStruct((128, 2048), F32),
        ),
        in_specs=[hbm],
        out_specs=(place, place),
        scratch_shapes=[
            buf(128, 2048), buf(8, N, 256), buf(8, 128, 256), buf(N, 128), buf(32, 8, 128), buf(3, 8, 128), buf(16, 8, 128), buf(32, 8, 128),
            buf(2, 4, N, 128), buf(2, N, 512), buf(2, 3, N, 128), buf(2, 48, 512), buf(2, 48, 512), buf(2, 48, 512),
            buf(2, N, 128), buf(2, 4, 48, 128), buf(2, 48, 128), buf(2, 48, 128), buf(2, 48, 128), buf(2, 3, 48, 128),
            buf(4, 4, 48, 128), buf(2, 4, N, 128), buf(2, 4, N, 128),
            buf(64, 64), buf(4, 64, 64), buf(N, N), buf(128, N),
            pltpu.SemaphoreType.DMA((7,)), pltpu.SemaphoreType.DMA((PANELS,)),
            pltpu.SemaphoreType.DMA((MESSAGES,)), pltpu.SemaphoreType.DMA((MESSAGES,)),
            pltpu.SemaphoreType.DMA((2,)), pltpu.SemaphoreType.DMA((16,)),
            pltpu.SemaphoreType.REGULAR, pltpu.SemaphoreType.REGULAR,
        ],
        compiler_params=pltpu.CompilerParams(
            collective_id=0, has_side_effects=True, vmem_limit_bytes=50 << 20
        ),
    )(slab)
    return pl.pallas_call(
        write_out,
        out_shape=(
            jax.ShapeDtypeStruct((N, 2048), F32),
            jax.ShapeDtypeStruct((128, 2048), F32),
        ),
        in_specs=[place, place],
        out_specs=(place, place),
        scratch_shapes=[pltpu.SemaphoreType.DMA((2,))],
        compiler_params=pltpu.CompilerParams(vmem_limit_bytes=8 << 20),
    )(*results)


def solution(mesh):
    return jax.shard_map(
        on_device,
        mesh=mesh,
        in_specs=(P("rows", "cols"),),
        out_specs=(P(None, "cols"), P("rows", "cols")),
        check_vma=False,
    )
```

```python
import functools
import math

import jax
import jax.numpy as jnp
from jax import lax
from jax.experimental import pallas as pl
from jax.experimental.pallas import tpu as pltpu
from jax.sharding import PartitionSpec as P

MESH = pl.DeviceIdType.MESH
PANEL = 64
PANELS = 3
N = PANEL * PANELS
F32 = jnp.float32


def dot(a, b, dims=((1,), (0,))):
    return lax.dot_general(
        a, b, (dims, ((), ())), precision=lax.Precision.HIGHEST, preferred_element_type=F32
    )


def dot_t(a, b):
    return dot(a, b, ((1,), (1,)))


def eliminate(s_ref):
    n = PANEL
    lane = lax.broadcasted_iota(jnp.int32, (n, n), 1)
    sub = lax.broadcasted_iota(jnp.int32, (n, n), 0)
    row_lane = lax.broadcasted_iota(jnp.int32, (1, n), 1)
    col_sub = lax.broadcasted_iota(jnp.int32, (n, 1), 0)

    def pick(value, where):
        return jnp.sum(jnp.where(where, value, 0.0), axis=1, keepdims=True)

    def step(i, _):
        j = 2 * i
        s = s_ref[...]
        r0 = s_ref[pl.ds(j, 1), :]
        r1 = s_ref[pl.ds(j + 1, 1), :]
        a = pick(r0, row_lane == j)
        b = pick(r1, row_lane == j)
        d = pick(r1, row_lane == j + 1)
        c0 = pick(s, lane == j)
        c1 = pick(s, lane == j + 1)
        a_inv = 1.0 / a
        ratio = b * a_inv
        second = d - b * ratio
        second_inv = 1.0 / second
        r0m = jnp.where(row_lane == j, 1.0, r0)
        r1n = jnp.where(row_lane == j, 0.0, r1) - ratio * r0m
        r0u = jnp.where(row_lane == j + 1, 0.0, r0m) * a_inv
        r1u = jnp.where(row_lane == j + 1, 1.0, r1n) * second_inv
        r1s = jnp.where(row_lane == j + 1, second, r1n)
        below = col_sub > j + 1
        c0b = jnp.where(below, c0, 0.0)
        c1b = jnp.where(below, c1 - c0 * ratio, 0.0)
        base = jnp.where((lane >= j) & (lane <= j + 1) & (sub > j + 1), 0.0, s)
        s_ref[...] = jnp.where(sub == j + 1, r1s, base - c0b * r0u - c1b * r1u)
        return 0

    lax.fori_loop(0, n // 2, step, 0)
    s = s_ref[...]
    pivots = pick(s, lane == sub)
    return jnp.where(lane < sub, s, jnp.where(lane == sub, 1.0, 0.0)) * (1.0 / jnp.sqrt(pivots))


def kernel(
    slab_hbm, r_out, u_out,
    slab, r_buf, u_buf, at, gp, g1, g2, gfull,
    mx, mz, rx1, rz1a, rz1b, rz1c, px, pz, rx2a, rx2b, rx2c, rz2, rr, mfx, mfz,
    s_ref, l_ref, t_ref, q_ref,
    p_send, p_recv, sends, recvs, in_sem, out_sem, far1, far2,
):
    row, col = lax.axis_index("rows"), lax.axis_index("cols")
    z, x = row // 4, row % 4
    zhi, zlo = z // 4, z % 4

    def at_z(dz):
        return (((z + dz + 16) % 16) * 4 + x, col)

    def at_x(d):
        return (z * 4 + (x + d) % 4, col)

    def at_col(d):
        return (row, (col + d) % 8)

    first = pltpu.make_async_copy(slab_hbm.at[:, 0:256], slab.at[:, 0:256], in_sem.at[0])
    rest = pltpu.make_async_copy(slab_hbm.at[:, 256:2048], slab.at[:, 256:2048], in_sem.at[1])
    first.start()
    rest.start()

    z_peers = (1, -1, 2, -2)
    peers = [at_z(d) for d in z_peers] + [at_x(d) for d in (1, 2, 3)] + [at_col(d) for d in range(1, 8)]
    barrier = pltpu.get_barrier_semaphore()
    for peer in peers:
        pl.semaphore_signal(barrier, inc=1, device_id=peer, device_id_type=MESH)
    pl.semaphore_wait(barrier, len(peers))
    for d in (2, -2):
        pl.semaphore_signal(far1, inc=1, device_id=at_z(d), device_id_type=MESH)
    first.wait()

    started = []

    def send(src, dst, peer):
        i = len(started)
        copy = pltpu.make_async_remote_copy(
            src_ref=src, dst_ref=dst, send_sem=sends.at[i], recv_sem=recvs.at[i],
            device_id=peer, device_id_type=MESH,
        )
        copy.start()
        started.append(copy)
        return copy

    def arrived(copies):
        for copy in copies:
            copy.wait_recv()

    def panel_copy(owner, d):
        rows = at.at[pl.ds(pl.multiple_of(owner * PANEL, PANEL), PANEL)]
        return pltpu.make_async_remote_copy(
            src_ref=rows, dst_ref=rows, send_sem=p_send.at[d - 1], recv_sem=p_recv.at[owner],
            device_id=at_col(d), device_id_type=MESH,
        )

    @pl.when(col < PANELS)
    def _():
        at[pl.ds(pl.multiple_of(col * PANEL, PANEL), PANEL), :] = slab[:, 0:128].T[:PANEL]
        for d in (4, 3, 5, 2, 6, 7, 1):
            panel_copy(col, d).start()

    pl.semaphore_wait(far1, 2)
    for d in (4, -4):
        pl.semaphore_signal(far2, inc=1, device_id=at_z(d), device_id_type=MESH)
    rest.wait()
    for k in range(PANELS):
        @pl.when(col != k)
        def _():
            panel_copy(k, 1).wait_recv()

    panels_t = at[...]

    gp[0:24] = dot_t(panels_t, panels_t[0:128]).reshape(24, 8, 128)
    gp[24:32] = dot_t(panels_t[128:192], jnp.concatenate([panels_t[128:192], panels_t[128:192]], 0)).reshape(8, 8, 128)
    mine = 4 * col + x
    c_g1 = [send(gp.at[4 * col + (x + d) % 4], g1.at[d - 1], at_x(d)) for d in (2, 1, 3)]

    def around_z(piece, half_a, half_b, dst, dst_a, dst_b):
        far = (zlo + 2) % 4
        return [
            send(half_a(far), dst_a, at_z(2)),
            send(half_b(far), dst_b, at_z(-2)),
            send(piece((zlo + 1) % 4), dst[0], at_z(1)),
            send(piece((zlo + 3) % 4), dst[1], at_z(-1)),
        ]

    def rows48(i):
        return pl.ds(pl.multiple_of(48 * i, 8), 48)

    def rows24(i, half):
        return pl.ds(pl.multiple_of(48 * i + 24 * half, 8), 24)

    def x_products(h):
        m = dot(panels_t, slab[:, 512 * h:512 * h + 512])
        for q in range(4):
            mx[h, q] = m[:, 128 * q:128 * q + 128]

    def z_products(h):
        mz[h] = dot(panels_t, slab[:, 1024 + 512 * h:1536 + 512 * h])

    def x1(h):
        return [send(mx.at[h, (x + d) % 4], rx1.at[h, d - 1], at_x(d)) for d in (2, 1, 3)]

    def z1(h):
        return around_z(
            lambda i: mz.at[h, rows48(i)], lambda i: mz.at[h, rows24(i, 0)], lambda i: mz.at[h, rows24(i, 1)],
            (rz1a.at[h], rz1b.at[h]), rz1c.at[h, 0:24], rz1c.at[h, 24:48],
        )

    def x2(h, before):
        arrived(before)
        px[h] = mx[h, x] + rx1[h, 0] + rx1[h, 1] + rx1[h, 2]
        return around_z(
            lambda i: px.at[h, rows48(i)], lambda i: px.at[h, rows24(i, 0)], lambda i: px.at[h, rows24(i, 1)],
            (rx2a.at[h], rx2b.at[h]), rx2c.at[h, 0:24], rx2c.at[h, 24:48],
        )

    def z2(h, before):
        arrived(before)
        for q in range(4):
            cols = slice(128 * q, 128 * q + 128)
            pz[h, q] = mz[h, rows48(zlo), cols] + rz1a[h, :, cols] + rz1b[h, :, cols] + rz1c[h, :, cols]
        return [send(pz.at[h, (x + d) % 4], rz2.at[h, d - 1], at_x(d)) for d in (2, 1, 3)]

    def across_z(s):
        return [send(rr.at[s, zhi], rr.at[s, zhi], at_z(4 * e)) for e in (2, 1, 3)]

    def x3(h, before):
        arrived(before)
        rr[h, zhi] = px[h, rows48(zlo), :] + rx2a[h] + rx2b[h] + rx2c[h]
        return across_z(h)

    def z3(h, before):
        arrived(before)
        rr[2 + h, zhi] = pz[h, x] + rz2[h, 0] + rz2[h, 1] + rz2[h, 2]
        return across_z(2 + h)

    def own_rows(ref, at_rows):
        whole, half_a, half_b = (at_rows(ref, rows) for rows in (rows48(zlo), rows24(zlo, 0), rows24(zlo, 1)))
        return around_z(
            lambda i: whole, lambda i: half_a, lambda i: half_b, (whole, whole), half_a, half_b
        )

    def x4(h, before):
        arrived(before)
        mfx[h, x, rows48(zlo), :] = rr[h, 0] + rr[h, 1] + rr[h, 2] + rr[h, 3]
        return own_rows(mfx.at[h, x], lambda ref, rows: ref.at[rows])

    def z4(h, before):
        arrived(before)
        mfz[h, x, rows48(zlo), :] = rr[2 + h, 0] + rr[2 + h, 1] + rr[2 + h, 2] + rr[2 + h, 3]
        own = mfz.at[h, x, rows48(zlo)]
        return [send(own, own, at_x(d)) for d in (2, 1, 3)]

    def z5(h, before):
        arrived(before)
        return own_rows(mfz.at[h], lambda ref, rows: ref.at[:, rows])

    z_products(0)
    c_z1 = [z1(0)]
    x_products(0)
    c_x1 = [x1(0)]
    x_products(1)
    c_x1.append(x1(1))
    z_products(1)
    arrived(c_g1)
    g2[z] = gp[mine] + g1[0] + g1[1] + g1[2]
    pl.semaphore_wait(far2, 2)
    c_g2 = [send(g2.at[z], g2.at[z], at_z(d)) for d in (8, 7, 9, 6, 10, 5, 11, 4, 12, 3, 13, 2, 14, 1, 15)]
    c_z1.append(z1(1))

    c_z2 = [z2(0, c_z1[0])]
    c_x2 = [x2(0, c_x1[0])]
    c_x2.append(x2(1, c_x1[1]))
    arrived(c_g2)
    total = g2[0]
    for i in range(1, 16):
        total = total + g2[i]
    gfull[mine] = total
    c_g4 = [send(gfull.at[mine], gfull.at[mine], at_x(d)) for d in (2, 1, 3)]
    c_z3 = [z3(0, c_z2[0])]
    c_z2.append(z2(1, c_z1[1]))
    c_x3 = [x3(0, c_x2[0])]
    arrived(c_g4)
    four = gfull.at[pl.ds(4 * col, 4)]
    c_g5 = [send(four, four, at_col(d)) for d in (4, 3, 5, 2, 6, 7, 1)]
    c_x3.append(x3(1, c_x2[1]))
    c_z3.append(z3(1, c_z2[1]))
    arrived(c_g5)

    def block(i, j):
        if j == 2:
            return gfull[24:32].reshape(64, 128)[:, 0:64]
        return gfull[8 * i:8 * i + 8].reshape(64, 128)[:, 64 * j:64 * j + 64]

    t_ref[...] = jnp.zeros_like(t_ref)
    s_ref[...] = block(0, 0)
    t00 = eliminate(s_ref)
    l10, l20 = dot_t(block(1, 0), t00), dot_t(block(2, 0), t00)
    t_ref[0:64, 0:64] = t00
    l_ref[0], l_ref[1] = l10, l20
    s_ref[...] = block(1, 1) - dot_t(l10, l10)
    l_ref[2] = block(2, 1) - dot_t(l20, l10)
    l_ref[3] = block(2, 2) - dot_t(l20, l20)

    c_z4 = [z4(0, c_z3[0])]

    t11 = eliminate(s_ref)
    t_ref[64:128, 64:128] = t11
    l21 = dot_t(l_ref[2], t11)
    l_ref[2] = l21
    s_ref[...] = l_ref[3] - dot_t(l21, l21)

    c_x4 = [x4(0, c_x3[0])]

    t_ref[128:192, 128:192] = eliminate(s_ref)

    c_x4.append(x4(1, c_x3[1]))
    c_z4.append(z4(1, c_z3[1]))
    arrived(c_x4[0])
    c_x5 = [[send(mfx.at[0, x], mfx.at[0, x], at_x(d)) for d in (2, 1, 3)]]
    c_z5 = [z5(0, c_z4[0])]
    arrived(c_x4[1])
    c_x5.append([send(mfx.at[1, x], mfx.at[1, x], at_x(d)) for d in (2, 1, 3)])

    t00, t11, t22 = (t_ref[i:i + 64, i:i + 64] for i in (0, 64, 128))
    l10, l20, l21 = l_ref[0], l_ref[1], l_ref[2]
    t10 = -dot(t11, dot(l10, t00))
    t_ref[64:128, 0:64] = t10
    t_ref[128:192, 0:64] = -dot(t22, dot(l20, t00) + dot(l21, t10))
    t_ref[128:192, 64:128] = -dot(t22, dot(l21, t11))
    q_ref[...] = dot(t_ref[...], at[...]).T

    norm_scale = 1.0 / math.sqrt(128 * 64)

    c_z5.append(z5(1, c_z4[1]))
    outs = []

    def finish(coeffs, first):
        i = len(outs) // 2
        cols = pl.ds(first, 256)
        r_buf[i] = coeffs * norm_scale
        outs.append(pltpu.make_async_copy(r_buf.at[i], r_out.at[:, cols], out_sem.at[2 * i]))
        outs[-1].start()
        u_buf[i] = slab[:, cols] - dot(q_ref[...], coeffs)
        outs.append(pltpu.make_async_copy(u_buf.at[i], u_out.at[:, cols], out_sem.at[2 * i + 1]))
        outs[-1].start()

    def finish_all(before, products, first):
        arrived(before)
        for q in (0, 2):
            pair = jnp.concatenate([products[q], products[q + 1]], 1)
            finish(dot(t_ref[...], pair), first + 128 * q)

    finish_all(c_x5[0], mfx.at[0], 0)
    finish_all(c_z5[0], mfz.at[0], 1024)
    finish_all(c_x5[1], mfx.at[1], 512)
    finish_all(c_z5[1], mfz.at[1], 1536)

    for copy in outs:
        copy.wait()
    for copy in started:
        copy.wait_send()

    @pl.when(col < PANELS)
    def _():
        for d in range(1, 8):
            panel_copy(col, d).wait_send()


def write_out(r_in, u_in, r_out, u_out, sems):
    copies = [
        pltpu.make_async_copy(r_in, r_out, sems.at[0]),
        pltpu.make_async_copy(u_in, u_out, sems.at[1]),
    ]
    for copy in copies:
        copy.start()
    for copy in copies:
        copy.wait()


MESSAGES = 96


def on_device(slab):
    hbm = pl.BlockSpec(memory_space=pltpu.HBM)
    place = pl.BlockSpec(memory_space=pl.ANY)

    def buf(*shape):
        return pltpu.VMEM(shape, F32)

    results = pl.pallas_call(
        kernel,
        out_shape=(
            jax.ShapeDtypeStruct((N, 2048), F32),
            jax.ShapeDtypeStruct((128, 2048), F32),
        ),
        in_specs=[hbm],
        out_specs=(place, place),
        scratch_shapes=[
            buf(128, 2048), buf(8, N, 256), buf(8, 128, 256), buf(N, 128), buf(32, 8, 128), buf(3, 8, 128), buf(16, 8, 128), buf(32, 8, 128),
            buf(2, 4, N, 128), buf(2, N, 512), buf(2, 3, N, 128), buf(2, 48, 512), buf(2, 48, 512), buf(2, 48, 512),
            buf(2, N, 128), buf(2, 4, 48, 128), buf(2, 48, 128), buf(2, 48, 128), buf(2, 48, 128), buf(2, 3, 48, 128),
            buf(4, 4, 48, 128), buf(2, 4, N, 128), buf(2, 4, N, 128),
            buf(64, 64), buf(4, 64, 64), buf(N, N), buf(128, N),
            pltpu.SemaphoreType.DMA((7,)), pltpu.SemaphoreType.DMA((PANELS,)),
            pltpu.SemaphoreType.DMA((MESSAGES,)), pltpu.SemaphoreType.DMA((MESSAGES,)),
            pltpu.SemaphoreType.DMA((2,)), pltpu.SemaphoreType.DMA((16,)),
            pltpu.SemaphoreType.REGULAR, pltpu.SemaphoreType.REGULAR,
        ],
        compiler_params=pltpu.CompilerParams(
            collective_id=0, has_side_effects=True, vmem_limit_bytes=50 << 20
        ),
    )(slab)
    return pl.pallas_call(
        write_out,
        out_shape=(
            jax.ShapeDtypeStruct((N, 2048), F32),
            jax.ShapeDtypeStruct((128, 2048), F32),
        ),
        in_specs=[place, place],
        out_specs=(place, place),
        scratch_shapes=[pltpu.SemaphoreType.DMA((2,))],
        compiler_params=pltpu.CompilerParams(vmem_limit_bytes=8 << 20),
    )(*results)


def solution(mesh):
    return jax.shard_map(
        on_device,
        mesh=mesh,
        in_specs=(P("rows", "cols"),),
        out_specs=(P(None, "cols"), P("rows", "cols")),
        check_vma=False,
    )
```

```python
import functools
import math

import jax
import jax.numpy as jnp
from jax import lax
from jax.experimental import pallas as pl
from jax.experimental.pallas import tpu as pltpu
from jax.sharding import PartitionSpec as P

MESH = pl.DeviceIdType.MESH
PANEL = 64
PANELS = 3
N = PANEL * PANELS
F32 = jnp.float32


def dot(a, b, dims=((1,), (0,))):
    return lax.dot_general(
        a, b, (dims, ((), ())), precision=lax.Precision.HIGHEST, preferred_element_type=F32
    )


def dot_t(a, b):
    return dot(a, b, ((1,), (1,)))


def eliminate(s_ref):
    n = PANEL
    lane = lax.broadcasted_iota(jnp.int32, (n, n), 1)
    sub = lax.broadcasted_iota(jnp.int32, (n, n), 0)
    row_lane = lax.broadcasted_iota(jnp.int32, (1, n), 1)
    col_sub = lax.broadcasted_iota(jnp.int32, (n, 1), 0)

    def pick(value, where):
        return jnp.sum(jnp.where(where, value, 0.0), axis=1, keepdims=True)

    def step(i, _):
        j = 2 * i
        s = s_ref[...]
        r0 = s_ref[pl.ds(j, 1), :]
        r1 = s_ref[pl.ds(j + 1, 1), :]
        a = pick(r0, row_lane == j)
        b = pick(r1, row_lane == j)
        d = pick(r1, row_lane == j + 1)
        c0 = pick(s, lane == j)
        c1 = pick(s, lane == j + 1)
        a_inv = 1.0 / a
        ratio = b * a_inv
        second = d - b * ratio
        second_inv = 1.0 / second
        r0m = jnp.where(row_lane == j, 1.0, r0)
        r1n = jnp.where(row_lane == j, 0.0, r1) - ratio * r0m
        r0u = jnp.where(row_lane == j + 1, 0.0, r0m) * a_inv
        r1u = jnp.where(row_lane == j + 1, 1.0, r1n) * second_inv
        r1s = jnp.where(row_lane == j + 1, second, r1n)
        below = col_sub > j + 1
        c0b = jnp.where(below, c0, 0.0)
        c1b = jnp.where(below, c1 - c0 * ratio, 0.0)
        base = jnp.where((lane >= j) & (lane <= j + 1) & (sub > j + 1), 0.0, s)
        s_ref[...] = jnp.where(sub == j + 1, r1s, base - c0b * r0u - c1b * r1u)
        return 0

    lax.fori_loop(0, n // 2, step, 0)
    s = s_ref[...]
    pivots = pick(s, lane == sub)
    return jnp.where(lane < sub, s, jnp.where(lane == sub, 1.0, 0.0)) * (1.0 / jnp.sqrt(pivots))


def kernel(
    slab_hbm, r_out, u_out,
    slab, r_buf, u_buf, at, gp, g1, g2, gfull,
    mx, mz, rx1, rz1a, rz1b, rz1c, px, pz, rx2a, rx2b, rx2c, rz2, rr, mfx, mfz, cx,
    s_ref, l_ref, t_ref, q_ref,
    p_send, p_recv, sends, recvs, in_sem, out_sem, far1, far2,
):
    row, col = lax.axis_index("rows"), lax.axis_index("cols")
    z, x = row // 4, row % 4
    zhi, zlo = z // 4, z % 4

    def at_z(dz):
        return (((z + dz + 16) % 16) * 4 + x, col)

    def at_x(d):
        return (z * 4 + (x + d) % 4, col)

    def at_col(d):
        return (row, (col + d) % 8)

    first = pltpu.make_async_copy(slab_hbm.at[:, 0:256], slab.at[:, 0:256], in_sem.at[0])
    rest = pltpu.make_async_copy(slab_hbm.at[:, 256:2048], slab.at[:, 256:2048], in_sem.at[1])
    first.start()
    rest.start()

    z_peers = (1, -1, 2, -2)
    peers = [at_z(d) for d in z_peers] + [at_x(d) for d in (1, 2, 3)] + [at_col(d) for d in range(1, 8)]
    barrier = pltpu.get_barrier_semaphore()
    for peer in peers:
        pl.semaphore_signal(barrier, inc=1, device_id=peer, device_id_type=MESH)
    pl.semaphore_wait(barrier, len(peers))
    for d in (2, -2):
        pl.semaphore_signal(far1, inc=1, device_id=at_z(d), device_id_type=MESH)
    first.wait()

    started = []

    def send(src, dst, peer):
        i = len(started)
        copy = pltpu.make_async_remote_copy(
            src_ref=src, dst_ref=dst, send_sem=sends.at[i], recv_sem=recvs.at[i],
            device_id=peer, device_id_type=MESH,
        )
        copy.start()
        started.append(copy)
        return copy

    def arrived(copies):
        for copy in copies:
            copy.wait_recv()

    def panel_copy(owner, d):
        rows = at.at[pl.ds(pl.multiple_of(owner * PANEL, PANEL), PANEL)]
        return pltpu.make_async_remote_copy(
            src_ref=rows, dst_ref=rows, send_sem=p_send.at[d - 1], recv_sem=p_recv.at[owner],
            device_id=at_col(d), device_id_type=MESH,
        )

    @pl.when(col < PANELS)
    def _():
        at[pl.ds(pl.multiple_of(col * PANEL, PANEL), PANEL), :] = slab[:, 0:128].T[:PANEL]
        for d in (4, 3, 5, 2, 6, 7, 1):
            panel_copy(col, d).start()

    pl.semaphore_wait(far1, 2)
    for d in (4, -4):
        pl.semaphore_signal(far2, inc=1, device_id=at_z(d), device_id_type=MESH)
    rest.wait()
    for k in range(PANELS):
        @pl.when(col != k)
        def _():
            panel_copy(k, 1).wait_recv()

    panels_t = at[...]

    gp[0:24] = dot_t(panels_t, panels_t[0:128]).reshape(24, 8, 128)
    gp[24:32] = dot_t(panels_t[128:192], jnp.concatenate([panels_t[128:192], panels_t[128:192]], 0)).reshape(8, 8, 128)
    mine = 4 * col + x
    c_g1 = [send(gp.at[4 * col + (x + d) % 4], g1.at[d - 1], at_x(d)) for d in (2, 1, 3)]

    def around_z(piece, half_a, half_b, dst, dst_a, dst_b):
        far = (zlo + 2) % 4
        return [
            send(half_a(far), dst_a, at_z(2)),
            send(half_b(far), dst_b, at_z(-2)),
            send(piece((zlo + 1) % 4), dst[0], at_z(1)),
            send(piece((zlo + 3) % 4), dst[1], at_z(-1)),
        ]

    def rows48(i):
        return pl.ds(pl.multiple_of(48 * i, 8), 48)

    def rows24(i, half):
        return pl.ds(pl.multiple_of(48 * i + 24 * half, 8), 24)

    def x_products(h):
        m = dot(panels_t, slab[:, 512 * h:512 * h + 512])
        for q in range(4):
            mx[h, q] = m[:, 128 * q:128 * q + 128]

    def z_products(h):
        mz[h] = dot(panels_t, slab[:, 1024 + 512 * h:1536 + 512 * h])

    def x1(h):
        return [send(mx.at[h, (x + d) % 4], rx1.at[h, d - 1], at_x(d)) for d in (2, 1, 3)]

    def z1(h):
        return around_z(
            lambda i: mz.at[h, rows48(i)], lambda i: mz.at[h, rows24(i, 0)], lambda i: mz.at[h, rows24(i, 1)],
            (rz1a.at[h], rz1b.at[h]), rz1c.at[h, 0:24], rz1c.at[h, 24:48],
        )

    def x2(h, before):
        arrived(before)
        px[h] = mx[h, x] + rx1[h, 0] + rx1[h, 1] + rx1[h, 2]
        return around_z(
            lambda i: px.at[h, rows48(i)], lambda i: px.at[h, rows24(i, 0)], lambda i: px.at[h, rows24(i, 1)],
            (rx2a.at[h], rx2b.at[h]), rx2c.at[h, 0:24], rx2c.at[h, 24:48],
        )

    def z2(h, before):
        arrived(before)
        for q in range(4):
            cols = slice(128 * q, 128 * q + 128)
            pz[h, q] = mz[h, rows48(zlo), cols] + rz1a[h, :, cols] + rz1b[h, :, cols] + rz1c[h, :, cols]
        return [send(pz.at[h, (x + d) % 4], rz2.at[h, d - 1], at_x(d)) for d in (2, 1, 3)]

    def across_z(s):
        return [send(rr.at[s, zhi], rr.at[s, zhi], at_z(4 * e)) for e in (2, 1, 3)]

    def x3(h, before):
        arrived(before)
        rr[h, zhi] = px[h, rows48(zlo), :] + rx2a[h] + rx2b[h] + rx2c[h]
        return across_z(h)

    def z3(h, before):
        arrived(before)
        rr[2 + h, zhi] = pz[h, x] + rz2[h, 0] + rz2[h, 1] + rz2[h, 2]
        return across_z(2 + h)

    def own_rows(ref, at_rows):
        whole, half_a, half_b = (at_rows(ref, rows) for rows in (rows48(zlo), rows24(zlo, 0), rows24(zlo, 1)))
        return around_z(
            lambda i: whole, lambda i: half_a, lambda i: half_b, (whole, whole), half_a, half_b
        )

    def x4(h, before):
        arrived(before)
        mfx[h, x, rows48(zlo), :] = rr[h, 0] + rr[h, 1] + rr[h, 2] + rr[h, 3]
        return own_rows(mfx.at[h, x], lambda ref, rows: ref.at[rows])

    def z4(h, before):
        arrived(before)
        mfz[h, x, rows48(zlo), :] = rr[2 + h, 0] + rr[2 + h, 1] + rr[2 + h, 2] + rr[2 + h, 3]
        own = mfz.at[h, x, rows48(zlo)]
        return [send(own, own, at_x(d)) for d in (2, 1, 3)]

    def z5(h, before, chunks):
        arrived(before)
        return own_rows(mfz.at[h, chunks], lambda ref, rows: ref.at[:, rows])

    z_products(0)
    c_z1 = [z1(0)]
    x_products(0)
    c_x1 = [x1(0)]
    x_products(1)
    c_x1.append(x1(1))
    z_products(1)
    arrived(c_g1)
    g2[z] = gp[mine] + g1[0] + g1[1] + g1[2]
    pl.semaphore_wait(far2, 2)
    c_g2 = [send(g2.at[z], g2.at[z], at_z(d)) for d in (8, 7, 9, 6, 10, 5, 11, 4, 12, 3, 13, 2, 14, 1, 15)]
    c_z1.append(z1(1))

    c_z2 = [z2(0, c_z1[0])]
    c_x2 = [x2(0, c_x1[0])]
    c_x2.append(x2(1, c_x1[1]))
    arrived(c_g2)
    total = g2[0]
    for i in range(1, 16):
        total = total + g2[i]
    gfull[mine] = total
    c_g4 = [send(gfull.at[mine], gfull.at[mine], at_x(d)) for d in (2, 1, 3)]
    c_z3 = [z3(0, c_z2[0])]
    c_z2.append(z2(1, c_z1[1]))
    c_x3 = [x3(0, c_x2[0])]
    arrived(c_g4)
    four = gfull.at[pl.ds(4 * col, 4)]
    c_g5 = [send(four, four, at_col(d)) for d in (4, 3, 5, 2, 6, 7, 1)]
    c_x3.append(x3(1, c_x2[1]))
    c_z3.append(z3(1, c_z2[1]))
    arrived(c_g5)

    def block(i, j):
        if j == 2:
            return gfull[24:32].reshape(64, 128)[:, 0:64]
        return gfull[8 * i:8 * i + 8].reshape(64, 128)[:, 64 * j:64 * j + 64]

    t_ref[...] = jnp.zeros_like(t_ref)
    s_ref[...] = block(0, 0)
    t00 = eliminate(s_ref)
    l10, l20 = dot_t(block(1, 0), t00), dot_t(block(2, 0), t00)
    t_ref[0:64, 0:64] = t00
    l_ref[0], l_ref[1] = l10, l20
    s_ref[...] = block(1, 1) - dot_t(l10, l10)
    l_ref[2] = block(2, 1) - dot_t(l20, l10)
    l_ref[3] = block(2, 2) - dot_t(l20, l20)

    c_z4 = [z4(0, c_z3[0])]

    t11 = eliminate(s_ref)
    t_ref[64:128, 64:128] = t11
    l21 = dot_t(l_ref[2], t11)
    l_ref[2] = l21
    s_ref[...] = l_ref[3] - dot_t(l21, l21)

    c_x4 = [x4(0, c_x3[0])]

    t_ref[128:192, 128:192] = eliminate(s_ref)

    c_x4.append(x4(1, c_x3[1]))
    c_z4.append(z4(1, c_z3[1]))
    c_z5 = [z5(0, c_z4[0], slice(0, 4))]
    arrived(c_x4[0])
    c_x5 = [[send(mfx.at[0, x], mfx.at[0, x], at_x(d)) for d in (2, 1, 3)]]

    t00, t11, t22 = (t_ref[i:i + 64, i:i + 64] for i in (0, 64, 128))
    l10, l20, l21 = l_ref[0], l_ref[1], l_ref[2]
    t10 = -dot(t11, dot(l10, t00))
    t_ref[64:128, 0:64] = t10
    t_ref[128:192, 0:64] = -dot(t22, dot(l20, t00) + dot(l21, t10))
    t_ref[128:192, 64:128] = -dot(t22, dot(l21, t11))
    q_ref[...] = dot(t_ref[...], at[...]).T

    norm_scale = 1.0 / math.sqrt(128 * 64)

    arrived(c_x4[1])
    cx[x] = dot(t_ref[...], mfx[1, x])
    c_x5.append([send(cx.at[x], cx.at[x], at_x(d)) for d in (2, 1, 3)])
    c_z5.append(z5(1, c_z4[1], slice(0, 2)))
    c_z5.append(z5(1, [], slice(2, 4)))
    outs = []

    def finish(coeffs, first):
        i = len(outs) // 2
        cols = pl.ds(first, 256)
        r_buf[i] = coeffs * norm_scale
        outs.append(pltpu.make_async_copy(r_buf.at[i], r_out.at[:, cols], out_sem.at[2 * i]))
        outs[-1].start()
        u_buf[i] = slab[:, cols] - dot(q_ref[...], coeffs)
        outs.append(pltpu.make_async_copy(u_buf.at[i], u_out.at[:, cols], out_sem.at[2 * i + 1]))
        outs[-1].start()

    def finish_all(coeffs_of, chunks, first):
        for q in (0, 2):
            finish(coeffs_of(jnp.concatenate([chunks[q], chunks[q + 1]], 1)), first + 128 * q)

    def from_products(m):
        return dot(t_ref[...], m)

    arrived(c_z5[0])
    finish_all(from_products, [mfz[0, q] for q in range(4)], 1024)
    arrived(c_x5[0])
    finish_all(from_products, [mfx[0, q] for q in range(4)], 0)
    arrived(c_x5[1])
    finish_all(lambda coeffs: coeffs, [cx[q] for q in range(4)], 512)
    for q in (0, 2):
        arrived(c_z5[1 + q // 2])
        finish(from_products(jnp.concatenate([mfz[1, q], mfz[1, q + 1]], 1)), 1536 + 128 * q)

    for copy in outs:
        copy.wait()
    for copy in started:
        copy.wait_send()

    @pl.when(col < PANELS)
    def _():
        for d in range(1, 8):
            panel_copy(col, d).wait_send()


def write_out(r_in, u_in, r_out, u_out, sems):
    copies = [
        pltpu.make_async_copy(r_in, r_out, sems.at[0]),
        pltpu.make_async_copy(u_in, u_out, sems.at[1]),
    ]
    for copy in copies:
        copy.start()
    for copy in copies:
        copy.wait()


MESSAGES = 100


def on_device(slab):
    hbm = pl.BlockSpec(memory_space=pltpu.HBM)
    place = pl.BlockSpec(memory_space=pl.ANY)

    def buf(*shape):
        return pltpu.VMEM(shape, F32)

    results = pl.pallas_call(
        kernel,
        out_shape=(
            jax.ShapeDtypeStruct((N, 2048), F32),
            jax.ShapeDtypeStruct((128, 2048), F32),
        ),
        in_specs=[hbm],
        out_specs=(place, place),
        scratch_shapes=[
            buf(128, 2048), buf(8, N, 256), buf(8, 128, 256), buf(N, 128), buf(32, 8, 128), buf(3, 8, 128), buf(16, 8, 128), buf(32, 8, 128),
            buf(2, 4, N, 128), buf(2, N, 512), buf(2, 3, N, 128), buf(2, 48, 512), buf(2, 48, 512), buf(2, 48, 512),
            buf(2, N, 128), buf(2, 4, 48, 128), buf(2, 48, 128), buf(2, 48, 128), buf(2, 48, 128), buf(2, 3, 48, 128),
            buf(4, 4, 48, 128), buf(2, 4, N, 128), buf(2, 4, N, 128), buf(4, N, 128),
            buf(64, 64), buf(4, 64, 64), buf(N, N), buf(128, N),
            pltpu.SemaphoreType.DMA((7,)), pltpu.SemaphoreType.DMA((PANELS,)),
            pltpu.SemaphoreType.DMA((MESSAGES,)), pltpu.SemaphoreType.DMA((MESSAGES,)),
            pltpu.SemaphoreType.DMA((2,)), pltpu.SemaphoreType.DMA((16,)),
            pltpu.SemaphoreType.REGULAR, pltpu.SemaphoreType.REGULAR,
        ],
        compiler_params=pltpu.CompilerParams(
            collective_id=0, has_side_effects=True, vmem_limit_bytes=50 << 20
        ),
    )(slab)
    return pl.pallas_call(
        write_out,
        out_shape=(
            jax.ShapeDtypeStruct((N, 2048), F32),
            jax.ShapeDtypeStruct((128, 2048), F32),
        ),
        in_specs=[place, place],
        out_specs=(place, place),
        scratch_shapes=[pltpu.SemaphoreType.DMA((2,))],
        compiler_params=pltpu.CompilerParams(vmem_limit_bytes=8 << 20),
    )(*results)


def solution(mesh):
    return jax.shard_map(
        on_device,
        mesh=mesh,
        in_specs=(P("rows", "cols"),),
        out_specs=(P(None, "cols"), P("rows", "cols")),
        check_vma=False,
    )
```
